512 devices in a mesh: dp: 16 (over z_lo, core), ctx: 32 (over z_hi, y, x).
Axes of the slice: x: 4, y: 4, z: 16 (z_hi: 2, z_lo: 8; z = z_hi * 8 + z_lo), core: 2. Of those that a mesh axis runs over, the one named last changes fastest.
Arguments:
- stored_memory: bfloat16 [32, 16384, 1024], P('dp', 'ctx'), may hold values from -4 to 4
- opening_probe_vectors: bfloat16 [32, 256, 2048], P('dp', 'ctx'), may hold values from -128 to 128
- opening_memory_pairs: bfloat16 [32, 256, 1024], P('dp', 'ctx'), may hold values from -4 to 4
- opening_hidden_marks: int32 [32, 256], P('dp', 'ctx'), may hold values 0 or 1
- second_probe_vectors: bfloat16 [16, 256, 2048], P('dp', 'ctx'), may hold values from -128 to 128
- second_memory_pairs: bfloat16 [16, 256, 1024], P('dp', 'ctx'), may hold values from -4 to 4
- second_hidden_marks: int32 [16, 256], P('dp', 'ctx'), may hold values from 0 to 1, as said below
- continuing_sequence_ids: int32 [16], replicated, may hold values from 0 to 31, as said below
- blank_symbol_probe: bfloat16 [2048], replicated, may hold values from -15 to 15
- blank_symbol_pairs: bfloat16 [1024], replicated, may hold values from -4 to 4
Outputs:
- first_out: bfloat16 [32, 256, 2048], P('dp', 'ctx')
- second_focus_result: bfloat16 [16, 256, 2048], P('dp', 'ctx')
The draws below stay inside these ranges and needn't reach their ends.
Inputs may be any that keep to these rules, and one draw needn't show every extreme that they name: `continuing_sequence_ids`: distinct sequence numbers; slot j belongs to data group j, sequence n to data group n // 2. `second_hidden_marks`: every slot has at least one masked position.
All inputs are finite; a program needn't handle non-finite values. No bound on the sum of `opening_hidden_marks` on one device may be relied on, other than what follows from the above.
Results may differ from the reference program's by a relative error of at most 0.0075.
Values may be sent and summed in bfloat16 or wider, within the bound.
No kernel may reach another device: no remote copies, remote signals or barrier semaphores. Data moves between devices by JAX's collectives and lax.ppermute only.
A program may use at most 64 MiB of HBM per device.

```python
import math
import jax
import jax.numpy as jnp
from jax import lax

QH = 16
KVH = 4
HD = 128
BLOCK = 256
SEQ_GRP = 2
SEQS = 32
SLOTS = 16
CONTEXT = 16384


def anchor_parts(key):
    key = jax.random.fold_in(key, 101)
    pick_spot, pick_row, pick_key = jax.random.split(key, 3)
    stride = CONTEXT // 8
    spots = jnp.arange(4, dtype=jnp.int32)[None, :] * stride + jax.random.randint(pick_spot, (SEQS, 4), 0, stride)
    band = BLOCK // 4
    rows = jnp.arange(4, dtype=jnp.int32)[None, :] * band + jax.random.randint(pick_row, (SEQS, 4), 0, band)
    anchors = jax.random.uniform(pick_key, (SEQS, 4, KVH * HD), jnp.float32, -1.7, 1.7)
    return (spots, rows, anchors)


def place_target(order, where, target):
    found = jnp.argmax((order == target).astype(jnp.int32)).astype(jnp.int32)
    previous = order[where]
    order = order.at[found].set(previous)
    return order.at[where].set(target)


def chosen_slots(key):
    key = jax.random.fold_in(key, 202)
    pick_order, pick_start, pick_member = jax.random.split(key, 3)
    count = SLOTS
    order = jax.random.permutation(pick_order, count).astype(jnp.int32)
    first_slot = jax.random.randint(pick_start, (), 0, count).astype(jnp.int32)
    order = place_target(order, first_slot, (first_slot + count // 2) % count)
    other_slot = (first_slot + count // 2) % count
    order = place_target(order, other_slot, (other_slot + 1) % count)
    members = jax.random.randint(pick_member, (count,), 0, SEQ_GRP).astype(jnp.int32)
    return (order * SEQ_GRP + members).astype(jnp.int32)


def anchored_queries(base, rows, anchors, place_occupants, strength):
    count = base.shape[0]
    group_size = QH // KVH
    own_rows = rows[place_occupants]
    own_anchors = anchors[place_occupants].reshape(count, 4, KVH, 1, HD)
    tiled = jnp.broadcast_to(own_anchors, (count, 4, KVH, group_size, HD)).reshape(count, 4, QH * HD)
    factors = jnp.array([0.44, 0.68, 1.0, 1.0], dtype=jnp.float32) * strength / (0.96 * math.sqrt(HD))
    placed = jnp.arange(count, dtype=jnp.int32)[:, None]
    return base.at[placed, own_rows].set(tiled * factors[None, :, None])


def draw_stored_memory(key, part):
    spots, rows, anchors = anchor_parts(key)
    key = jax.random.fold_in(key, 13)
    shape = (SEQS, CONTEXT, 2 * KVH * HD)
    base = jnp.clip(jax.random.normal(key, shape, jnp.float32), -4.0, 4.0)
    placed = jnp.arange(SEQS, dtype=jnp.int32)[:, None]
    base = base.at[placed, spots, :KVH * HD].set(anchors)
    base = base.at[placed, spots + CONTEXT // 2, :KVH * HD].set(0.99 * anchors)
    return base.astype(jnp.bfloat16)


def draw_opening_probe_vectors(key, part):
    spots, rows, anchors = anchor_parts(key)
    key = jax.random.fold_in(key, 11)
    shape = (SEQS, BLOCK, QH * HD)
    base = jnp.clip(3.0 * jax.random.normal(key, shape, jnp.float32), -15.0, 15.0)
    strength = 8.0
    return anchored_queries(base, rows, anchors, jnp.arange(SEQS, dtype=jnp.int32), strength).astype(jnp.bfloat16)


def draw_second_probe_vectors(key, part):
    spots, rows, anchors = anchor_parts(key)
    place_occupants = chosen_slots(key)
    key = jax.random.fold_in(key, 17)
    shape = (SLOTS, BLOCK, QH * HD)
    base = jnp.clip(3.0 * jax.random.normal(key, shape, jnp.float32), -15.0, 15.0)
    strength = 8.0
    return anchored_queries(base, rows, anchors, place_occupants, strength).astype(jnp.bfloat16)


def draw_continuing_sequence_ids(key, part):
    return chosen_slots(key)


def draw_second_hidden_marks(key, part):
    key = jax.random.fold_in(key, 19)
    pick_bits, pick_forced = jax.random.split(key)
    random_bits = jax.random.randint(pick_bits, (SLOTS, BLOCK), 0, 2)
    forced = jax.random.randint(pick_forced, (SLOTS, 1), 0, BLOCK)
    positions = jnp.arange(BLOCK, dtype=jnp.int32)[None, :]
    return jnp.maximum(random_bits, (positions == forced).astype(jnp.int32)).astype(jnp.int32)


def place_ends(drawn, rng, least, largest):
    spot = [jax.random.randint(jax.random.fold_in(rng, axis), (), 0, length) for axis, length in enumerate(drawn.shape)]
    longest = drawn.shape.index(max(drawn.shape))
    beside = spot[:longest] + [(spot[longest] + 1) % drawn.shape[longest]] + spot[longest + 1:]
    return drawn.at[tuple(spot)].set(least).at[tuple(beside)].set(largest)


def steps_of(rng, shape, cuts, low, largest):
    def one(dim, shards_of):
        heights = jax.random.uniform(jax.random.fold_in(jax.random.fold_in(rng, 6), dim), (shards_of,), jnp.float32, low / len(cuts), largest / len(cuts))
        return jnp.repeat(jnp.exp(heights), shape[dim] // shards_of).reshape((-1,) + (1,) * (len(shape) - dim - 1))

    level = one(*cuts[0])
    for cut in cuts[1:]:
        level = level * one(*cut)
    return level


def normal_values(own_key, dims, width, limit, cuts=(), kind=jnp.bfloat16):
    level = steps_of(own_key, dims, cuts, -0.22, 0.18) if cuts else 1.0
    result = jax.random.normal(own_key, dims, jnp.float32) * width * level
    return jnp.minimum(jnp.maximum(result, -limit), limit).astype(kind)


def setup_inputs(seed: int = 0) -> dict:
    keys = jax.random.split(jax.random.key(seed), 11)
    return {
        "stored_memory": draw_stored_memory(jax.random.fold_in(keys[10], 71), 0),
        "opening_probe_vectors": draw_opening_probe_vectors(jax.random.fold_in(keys[10], 71), 0),
        "opening_memory_pairs": normal_values(keys[2], (SEQS, BLOCK, 2 * KVH * HD), 1.0, 4.0, ((0, 16), (1, 32))),
        "opening_hidden_marks": place_ends((jax.random.randint(keys[3], (SEQS, BLOCK), 0, 2) < 1).astype(jnp.int32), jax.random.fold_in(keys[3], 1), 0, 1),
        "second_probe_vectors": draw_second_probe_vectors(jax.random.fold_in(keys[10], 71), 0),
        "second_memory_pairs": normal_values(keys[5], (SLOTS, BLOCK, 2 * KVH * HD), 1.0, 4.0, ((0, 16), (1, 32))),
        "second_hidden_marks": draw_second_hidden_marks(jax.random.fold_in(keys[10], 71), 0),
        "continuing_sequence_ids": draw_continuing_sequence_ids(jax.random.fold_in(keys[10], 71), 0),
        "blank_symbol_probe": normal_values(keys[8], (QH * HD,), 3.0, 15.0),
        "blank_symbol_pairs": normal_values(keys[9], (2 * KVH * HD,), 1.0, 4.0),
    }


def masked_rows(values, masked, filler):
    return jnp.where(masked[..., None] == 1, filler, values)


def attend_one(queries, context, block_rows):
    keys_all = jnp.concatenate([context, block_rows], axis=0)
    group_size = QH // KVH
    score_scale = HD ** -0.5
    head_outs = []
    for kv_head in range(KVH):
        query_part = queries[:, kv_head * group_size * HD:(kv_head + 1) * group_size * HD]
        query_part = query_part.reshape(BLOCK, group_size, HD).astype(jnp.float32)
        key_part = keys_all[:, kv_head * HD:(kv_head + 1) * HD].astype(jnp.float32)
        value_part = keys_all[:, (KVH + kv_head) * HD:(KVH + kv_head + 1) * HD].astype(jnp.float32)
        scores = jnp.einsum("tjd,kd->tjk", query_part, key_part) * score_scale
        row_max = jnp.max(scores, axis=-1, keepdims=True)
        raised = jnp.exp(scores - row_max)
        row_total = jnp.sum(raised, axis=-1)
        weights = lax.optimization_barrier(raised.astype(jnp.bfloat16))
        blended = jnp.einsum("tjk,kd->tjd", weights.astype(jnp.float32), value_part)
        head_outs.append((blended / row_total[..., None]).reshape(BLOCK, group_size * HD))
    return jnp.concatenate(head_outs, axis=1).astype(jnp.bfloat16)


def reference(stored_memory, opening_probe_vectors, opening_memory_pairs, opening_hidden_marks, second_probe_vectors, second_memory_pairs, second_hidden_marks, continuing_sequence_ids, blank_symbol_probe, blank_symbol_pairs):
    query_first = masked_rows(opening_probe_vectors, opening_hidden_marks, blank_symbol_probe)
    block_first = masked_rows(opening_memory_pairs, opening_hidden_marks, blank_symbol_pairs)

    def sequence_attention(packed):
        return attend_one(packed[0], packed[1], packed[2])

    first_out = lax.map(sequence_attention, (query_first, stored_memory, block_first))
    probe_second_sweep = masked_rows(second_probe_vectors, second_hidden_marks, blank_symbol_probe)
    segment_second_sweep = masked_rows(second_memory_pairs, second_hidden_marks, blank_symbol_pairs)

    def each_place_focus(packed):
        context = lax.dynamic_index_in_dim(stored_memory, packed[2], 0, keepdims=False)
        return attend_one(packed[0], context, packed[1])

    second_focus_result = lax.map(each_place_focus, (probe_second_sweep, segment_second_sweep, continuing_sequence_ids))
    return first_out, second_focus_result
```

```python
import jax
import jax.numpy as jnp
from jax import lax
from jax.experimental import pallas as pl
from jax.experimental.pallas import tpu as pltpu
from jax.sharding import Mesh, PartitionSpec as P

QH = 16
KVH = 4
HD = 128
GRP = QH // KVH
GW = GRP * HD
ROWS = 8
PAY = GW + HD
DP = ("zl", "co")
PLANE = ("y", "x")
CTX = ("zh", "y", "x")
SCALE = HD ** -0.5
F32 = jnp.float32
BF16 = jnp.bfloat16


def cost(flops, nbytes, trans=0):
    return pl.CostEstimate(flops=flops, bytes_accessed=nbytes, transcendentals=trans)


def split_three(v):
    hi = v.astype(BF16)
    rest = v - hi.astype(F32)
    mid = rest.astype(BF16)
    low = (rest - mid.astype(F32)).astype(BF16)
    return hi.astype(F32), mid.astype(F32), low.astype(F32)


def cut_kernel(k_ref, v_ref, o_ref):
    o_ref[0, 0, :, :HD] = k_ref[0]
    o_ref[0, 0, :, HD:] = v_ref[0]


def cut_by_head(stored):
    seqs, rows, _ = stored.shape
    return pl.pallas_call(
        cut_kernel,
        grid=(KVH, seqs),
        in_specs=[
            pl.BlockSpec((1, rows, HD), lambda h, s: (s, 0, h)),
            pl.BlockSpec((1, rows, HD), lambda h, s: (s, 0, KVH + h)),
        ],
        out_specs=pl.BlockSpec((1, 1, rows, 2 * HD), lambda h, s: (h, s, 0, 0)),
        out_shape=jax.ShapeDtypeStruct((KVH, seqs, rows, 2 * HD), BF16),
        cost_estimate=cost(0, 4 * stored.size),
        name="cut_by_head",
    )(stored, stored)


def pack_kernel(own_ref, far_ref, kv_ref, o_ref):
    units = own_ref.shape[0]
    for u in range(units):
        for h in range(KVH):
            cols = slice(h * GW, (h + 1) * GW)
            q = jnp.concatenate(
                [own_ref[u, :, cols].astype(F32), far_ref[u, :, cols].astype(F32)], axis=0
            ).astype(BF16)
            k = kv_ref[u, :, h * HD:(h + 1) * HD].astype(F32)
            v = kv_ref[u, :, (KVH + h) * HD:(KVH + h + 1) * HD].astype(F32)
            kv = jnp.concatenate([k, v], axis=0).astype(BF16)
            for y in range(o_ref.shape[0] // KVH):
                o_ref[y * KVH + h, u, :, :GW] = q
                o_ref[y * KVH + h, u, :, GW:] = kv


def pack(own, far, kv):
    units = own.shape[0]
    places = lax.axis_size("y") * lax.axis_size("x")
    out = jax.ShapeDtypeStruct((places, units, 2 * ROWS, PAY), BF16)
    return pl.pallas_call(
        pack_kernel, out_shape=out, cost_estimate=cost(0, 2 * out.size), name="pack_queries"
    )(own, far, kv)


def attend_kernel(where_ref, q_ref, kv_ref, o_ref):
    places = q_ref.shape[0]
    rows = places * 2 * ROWS
    row_y = where_ref[where_ref.shape[0] - 1]
    near = q_ref[pl.ds(row_y * KVH, KVH), 0, :, GW:].astype(F32)
    kb = near[:, :ROWS].reshape(KVH * ROWS, HD).astype(BF16)
    vb = near[:, ROWS:].reshape(KVH * ROWS, HD).astype(BF16)
    lane = lax.broadcasted_iota(jnp.int32, (rows, HD), 1)
    stats = jnp.zeros((rows, HD), F32)
    nt = (((1,), (1,)), ((), ()))
    for j in range(GRP):
        q = q_ref[:, 0, :, j * HD:(j + 1) * HD].reshape(rows, HD)
        parts = [
            lax.dot_general(q, kv_ref[x, 0, :, :HD], nt, preferred_element_type=F32)
            for x in range(KVH)
        ]
        parts.append(lax.dot_general(q, kb, nt, preferred_element_type=F32))
        top = jnp.max(parts[0], axis=1, keepdims=True)
        for part in parts[1:]:
            top = jnp.maximum(top, jnp.max(part, axis=1, keepdims=True))
        total = jnp.zeros((rows, 1), F32)
        out = jnp.zeros((rows, HD), F32)
        for x, part in enumerate(parts):
            w = jnp.exp((part - top) * SCALE)
            total = total + jnp.sum(w, axis=1, keepdims=True)
            v = kv_ref[x, 0, :, HD:] if x < KVH else vb
            out = out + jnp.dot(w.astype(BF16), v, preferred_element_type=F32)
        o_ref[:, 0, :, j * HD:(j + 1) * HD] = (
            (out * (1.0 / total)).astype(BF16).reshape(places, 2 * ROWS, HD)
        )
        for i, piece in enumerate(split_three(top * SCALE + jnp.log(total))):
            stats = jnp.where(lane == i * GRP + j, piece, stats)
    o_ref[:, 0, :, GW:] = stats.astype(BF16).reshape(places, 2 * ROWS, HD)


def attend(where, queries, kv):
    places, units = queries.shape[:2]
    shape = (places, 1, 2 * ROWS, PAY)
    keys = kv.shape[0] * kv.shape[2]
    pairs = units * places * 2 * ROWS * GRP * keys
    return pl.pallas_call(
        attend_kernel,
        grid_spec=pltpu.PrefetchScalarGridSpec(
            num_scalar_prefetch=1,
            grid=(units,),
            in_specs=[
                pl.BlockSpec(shape, lambda u, w: (0, u, 0, 0)),
                pl.BlockSpec((KVH, 1) + kv.shape[2:], lambda u, w: (0, w[u], 0, 0)),
            ],
            out_specs=pl.BlockSpec(shape, lambda u, w: (0, u, 0, 0)),
        ),
        out_shape=jax.ShapeDtypeStruct(queries.shape, BF16),
        compiler_params=pltpu.CompilerParams(vmem_limit_bytes=48 * 2 ** 20),
        cost_estimate=cost(pairs * HD * 4, 4 * queries.size + 2 * kv.size, pairs),
        name="attend",
    )(where, queries, kv)


def merge(members):
    top = members[0][1]
    for _, lse in members[1:]:
        top = jnp.maximum(top, lse)
    total = 0.0
    out = 0.0
    for part, lse in members:
        w = jnp.exp(lse - top)
        total = total + w
        out = out + part * w
    return out * (1.0 / total), top + jnp.log(total)


def fold_kernel(r_ref, own_ref, lse_ref, far_ref):
    units = r_ref.shape[1]
    rows = 2 * ROWS
    lane = lax.broadcasted_iota(jnp.int32, (rows, HD), 1)
    for u in range(units):
        near = jnp.zeros((rows, HD), F32)
        sent = jnp.zeros((rows, HD), F32)
        for x in range(KVH):
            tails = []
            for y in range(r_ref.shape[0] // KVH):
                tail = r_ref[y * KVH + x, u, :, GW:].astype(F32)
                tails.append(
                    tail[:, :GRP] + tail[:, GRP:2 * GRP] + tail[:, 2 * GRP:3 * GRP]
                )
            for j in range(GRP):
                h = x * GRP + j
                out, lse = merge([
                    (r_ref[y * KVH + x, u, :, j * HD:(j + 1) * HD].astype(F32), t[:, j:j + 1])
                    for y, t in enumerate(tails)
                ])
                own_ref[u, :, h * HD:(h + 1) * HD] = out[:ROWS]
                far_ref[u, :, h * HD:(h + 1) * HD] = out[ROWS:].astype(BF16)
                near = jnp.where(lane == h, lse, near)
                for i, piece in enumerate(split_three(lse)):
                    sent = jnp.where(lane == i * QH + h, piece, sent)
        lse_ref[u] = near[:ROWS]
        far_ref[u, :, QH * HD:] = sent[ROWS:].astype(BF16)


def fold(received):
    units = received.shape[1]
    return pl.pallas_call(
        fold_kernel,
        out_shape=(
            jax.ShapeDtypeStruct((units, ROWS, QH * HD), F32),
            jax.ShapeDtypeStruct((units, ROWS, HD), F32),
            jax.ShapeDtypeStruct((units, ROWS, QH * HD + HD), BF16),
        ),
        cost_estimate=cost(0, 4 * received.size),
        name="fold_plane",
    )(received)


def finish_kernel(own_ref, lse_ref, far_ref, o_ref):
    for u in range(own_ref.shape[0]):
        tail = far_ref[u, :, QH * HD:].astype(F32)
        far_lse = tail[:, :QH] + tail[:, QH:2 * QH] + tail[:, 2 * QH:3 * QH]
        for h in range(QH):
            cols = slice(h * HD, (h + 1) * HD)
            out, _ = merge([
                (own_ref[u, :, cols], lse_ref[u, :, h:h + 1]),
                (far_ref[u, :, cols].astype(F32), far_lse[:, h:h + 1]),
            ])
            o_ref[u, :, cols] = out.astype(BF16)


def finish(own, lse, far):
    return pl.pallas_call(
        finish_kernel,
        out_shape=jax.ShapeDtypeStruct(own.shape, BF16),
        cost_estimate=cost(0, 8 * own.size),
        name="finish",
    )(own, lse, far)


def swap_halves(value):
    return lax.ppermute(value, "zh", [(0, 1), (1, 0)])


def exchange(value):
    return lax.all_to_all(value, PLANE, split_axis=0, concat_axis=0, tiled=True)


def masked_rows(values, masked, filler):
    return jnp.where(masked[..., None] == 1, filler, values)


def spread(queries, pairs):
    return exchange(pack(queries, swap_halves(queries), pairs))


def gather_back(partial):
    own, lse, far = fold(exchange(partial))
    return finish(own, lse, swap_halves(far))


def body(
    stored_memory,
    opening_probe_vectors,
    opening_memory_pairs,
    opening_hidden_marks,
    second_probe_vectors,
    second_memory_pairs,
    second_hidden_marks,
    continuing_sequence_ids,
    blank_symbol_probe,
    blank_symbol_pairs,
):
    seqs = stored_memory.shape[0]
    group = lax.axis_index("zl") * lax.axis_size("co") + lax.axis_index("co")
    groups = lax.axis_size("zl") * lax.axis_size("co")
    row_y = lax.axis_index("y").astype(jnp.int32)

    homes = continuing_sequence_ids // seqs
    slots = jnp.arange(groups, dtype=jnp.int32)
    earlier = (homes[None, :] == homes[:, None]) & (slots[None, :] < slots[:, None])
    rank = jnp.sum(earlier.astype(jnp.int32), axis=1)

    blanks = jnp.concatenate([blank_symbol_probe, blank_symbol_pairs])
    second = masked_rows(
        jnp.concatenate([second_probe_vectors, second_memory_pairs], axis=2),
        second_hidden_marks,
        blanks,
    )
    slot_rows = lax.all_gather(second, DP, axis=0, tiled=True)

    kv = lax.all_to_all(
        cut_by_head(stored_memory), "x", split_axis=0, concat_axis=0, tiled=True
    )

    query_first = masked_rows(opening_probe_vectors, opening_hidden_marks, blank_symbol_probe)
    block_first = masked_rows(opening_memory_pairs, opening_hidden_marks, blank_symbol_pairs)
    first_in = spread(query_first, block_first)
    where_first = jnp.concatenate([jnp.arange(seqs, dtype=jnp.int32), row_y[None]])
    first_out = gather_back(attend(where_first, first_in, kv))

    def second_pass(turn):
        mine = (homes == group) & (rank == turn)
        slot = jnp.argmax(mine).astype(jnp.int32)
        member = continuing_sequence_ids[slot] % seqs
        rows = lax.dynamic_slice_in_dim(slot_rows, slot, 1, 0)
        queries, pairs = rows[..., :QH * HD], rows[..., QH * HD:]
        where = jnp.stack([member, row_y])
        home_out = gather_back(attend(where, spread(queries, pairs), kv))
        every = lax.all_gather(home_out, DP, axis=0, tiled=True)
        return lax.dynamic_slice_in_dim(every, homes[group], 1, 0)

    result = second_pass(0)
    result = lax.cond(
        jnp.any(rank > 0),
        lambda early: jnp.where(rank[group] > 0, second_pass(1), early),
        lambda early: early,
        result,
    )
    return first_out, result


def solution(mesh):
    fine = Mesh(mesh.devices.reshape(8, 2, 2, 4, 4), ("zl", "co", "zh", "y", "x"))
    rows = P(DP, CTX, None)
    marks = P(DP, CTX)
    return jax.shard_map(
        body,
        mesh=fine,
        in_specs=(rows, rows, rows, marks, rows, rows, marks, P(), P(), P()),
        out_specs=(rows, rows),
        check_vma=False,
    )
```

```python
import functools

import jax
import jax.numpy as jnp
from jax import lax
from jax.experimental import pallas as pl
from jax.experimental.pallas import tpu as pltpu
from jax.sharding import Mesh, PartitionSpec as P

QH = 16
KVH = 4
HD = 128
GRP = QH // KVH
GW = GRP * HD
ROWS = 8
PAY = GW + HD
DP = ("zl", "co")
PLANE = ("y", "x")
CTX = ("zh", "y", "x")
SCALE = HD ** -0.5
F32 = jnp.float32
BF16 = jnp.bfloat16


def cost(flops, nbytes, trans=0):
    return pl.CostEstimate(flops=flops, bytes_accessed=nbytes, transcendentals=trans)


def params(mib):
    return pltpu.CompilerParams(vmem_limit_bytes=mib * 2 ** 20)


def shape(dims, dtype=BF16):
    return jax.ShapeDtypeStruct(dims, dtype)


def in_smem():
    return pl.BlockSpec(memory_space=pltpu.SMEM)


def in_vmem():
    return pl.BlockSpec(memory_space=pltpu.VMEM)


def split_three(v):
    hi = v.astype(BF16)
    rest = v - hi.astype(F32)
    mid = rest.astype(BF16)
    low = (rest - mid.astype(F32)).astype(BF16)
    return hi.astype(F32), mid.astype(F32), low.astype(F32)


SLOT, OTHER, MEMBER, HOME, HOME_OTHER = 0, 2, 4, 6, 7


def plan_kernel(seqs, ids_ref, o_ref):
    count = ids_ref.shape[0]
    core = lax.axis_index("co")
    group = lax.axis_index("zl") * lax.axis_size("co") + core
    other = group + 1 - 2 * core
    for where, place in ((group, SLOT), (other, OTHER)):
        seen = jnp.int32(0)
        slot = [jnp.int32(0), jnp.int32(0)]
        member = [jnp.int32(0), jnp.int32(0)]
        for j in range(count):
            one = ids_ref[j]
            home = lax.div(one, jnp.int32(seqs))
            hit = home == where
            for turn in range(2):
                now = hit & (seen == turn)
                slot[turn] = jnp.where(now, j, slot[turn])
                member[turn] = jnp.where(now, one - home * seqs, member[turn])
            seen = seen + hit.astype(jnp.int32)
        for turn in range(2):
            o_ref[place + turn] = slot[turn]
            if place == SLOT:
                o_ref[MEMBER + turn] = member[turn]
    o_ref[HOME] = lax.div(ids_ref[group], jnp.int32(seqs))
    o_ref[HOME_OTHER] = lax.div(ids_ref[other], jnp.int32(seqs))


def make_plan(ids, seqs):
    return pl.pallas_call(
        functools.partial(plan_kernel, seqs),
        in_specs=[in_smem()],
        out_specs=in_smem(),
        out_shape=shape((8,), jnp.int32),
        compiler_params=params(1),
        cost_estimate=cost(0, 128),
        name="plan",
    )(ids)


def head_of(y, x):
    return 2 * (y & 1) + (x & 1)


def own_head():
    return head_of(lax.axis_index("y"), lax.axis_index("x"))


def cut_kernel(s_ref, *outs):
    here = own_head()
    for d, out in enumerate(outs):
        head = jnp.bitwise_xor(here, d)
        for part in range(2):
            start = pl.multiple_of((part * KVH + head) * HD, HD)
            for n in range(out.shape[0]):
                out[n, :, part * HD:(part + 1) * HD] = s_ref[n, :, pl.ds(start, HD)]


def cut_by_head(stored):
    seqs, rows, _ = stored.shape
    return pl.pallas_call(
        cut_kernel,
        out_shape=[shape((seqs, rows, 2 * HD))] * KVH,
        compiler_params=params(12),
        cost_estimate=cost(0, 4 * stored.size),
        name="cut_by_head",
    )(stored)


def send_kernel(*refs):
    given, o_ref, held, sem = refs[:5], refs[5], refs[6:11], refs[11]
    copies = [pltpu.make_async_copy(a, b, sem.at[n]) for n, (a, b) in enumerate(zip(given, held))]
    for copy in copies:
        copy.start()
    for copy in copies:
        copy.wait()
    q_ref, kv_ref, mark_ref, bq_ref, bkv_ref = held
    square = (ROWS, ROWS)
    eye = lax.broadcasted_iota(jnp.int32, square, 0) == lax.broadcasted_iota(jnp.int32, square, 1)
    marks = jnp.broadcast_to(mark_ref[...], square)
    column = jnp.sum(jnp.where(eye, marks, 0).astype(F32), axis=1, keepdims=True)
    hidden = jnp.broadcast_to(column == 1.0, (ROWS, HD))
    for blank, values, first in ((bq_ref, q_ref, 0), (bkv_ref, kv_ref, q_ref.shape[2] // 2)):
        half = values.shape[2] // 2
        for c in range(2):
            value = jnp.concatenate(
                [
                    jnp.where(
                        hidden,
                        jnp.broadcast_to(blank[i:i + 1].astype(F32), (ROWS, HD)),
                        values[0, :, i * HD:(i + 1) * HD].astype(F32),
                    )
                    for i in range(c * half // HD, (c + 1) * half // HD)
                ],
                axis=1,
            ).astype(BF16)
            for chip in range(o_ref.shape[0] // 2):
                o_ref[2 * chip + c, :, first:first + half] = value


def send_slots(q, kv, marks, blank_q, blank_kv):
    groups = lax.axis_size("zl") * lax.axis_size("co")
    out = shape((groups, ROWS, (q.shape[2] + kv.shape[2]) // 2))
    given = (q, kv, marks, blank_q.reshape(-1, HD), blank_kv.reshape(-1, HD))
    return pl.pallas_call(
        send_kernel,
        in_specs=[pl.BlockSpec(memory_space=pltpu.HBM)] * len(given),
        out_specs=in_vmem(),
        out_shape=out,
        scratch_shapes=[pltpu.VMEM(value.shape, value.dtype) for value in given]
        + [pltpu.SemaphoreType.DMA((len(given),))],
        compiler_params=params(4),
        cost_estimate=cost(0, 2 * out.size),
        name="send_slots",
    )(*given)


def pick_kernel(entry, plan_ref, halves_ref, o_ref):
    o_ref[0] = halves_ref[plan_ref[entry]]


def pick(plan, halves, entry):
    return pl.pallas_call(
        functools.partial(pick_kernel, entry),
        in_specs=[in_smem(), in_vmem()],
        out_specs=in_vmem(),
        out_shape=shape((1,) + halves.shape[1:]),
        compiler_params=params(2),
        cost_estimate=cost(0, 4 * halves.size),
        name="pick",
    )(plan, halves)


def join_kernel(entry, given, plan_ref, halves_ref, got_ref, *refs):
    aheads, outs = refs[:given], refs[given:]
    kept = halves_ref[plan_ref[entry]]
    got = got_ref[0]
    low = lax.axis_index("co") == 0
    first = 0
    for n, out in enumerate(outs):
        last = out.shape[0] - 1
        if given:
            out[:last] = aheads[n][...]
        half = out.shape[2] // 2
        cols = slice(first, first + half)

        @pl.when(low)
        def _(out=out, last=last, half=half, cols=cols):
            out[last, :, :half] = kept[:, cols]
            out[last, :, half:] = got[:, cols]

        @pl.when(jnp.logical_not(low))
        def _(out=out, last=last, half=half, cols=cols):
            out[last, :, :half] = got[:, cols]
            out[last, :, half:] = kept[:, cols]

        first += half


def join(plan, halves, got, entry, widths, *aheads):
    units = 1 + (aheads[0].shape[0] if aheads else 0)
    return pl.pallas_call(
        functools.partial(join_kernel, entry, len(aheads)),
        in_specs=[in_smem()] + [in_vmem()] * (2 + len(aheads)),
        out_specs=[in_vmem()] * len(widths),
        out_shape=[shape((units, ROWS, width)) for width in widths],
        compiler_params=params(2),
        cost_estimate=cost(0, 4 * halves.size),
        name="join",
    )(plan, halves, got, *aheads)


def pack_kernel(own_ref, far_ref, kv_ref, o_ref):
    width = lax.axis_size("x")
    for u in range(own_ref.shape[0]):
        for h in range(KVH):
            cols = slice(h * GW, (h + 1) * GW)
            q = jnp.concatenate(
                [own_ref[u, :, cols].astype(F32), far_ref[u, :, cols].astype(F32)], axis=0
            ).astype(BF16)
            k = kv_ref[u, :, h * HD:(h + 1) * HD].astype(F32)
            v = kv_ref[u, :, (KVH + h) * HD:(KVH + h + 1) * HD].astype(F32)
            kv = jnp.concatenate([k, v], axis=0).astype(BF16)
            for place in range(o_ref.shape[0]):
                if head_of(place // width, place % width) == h:
                    o_ref[place, u, :, :GW] = q
                    o_ref[place, u, :, GW:] = kv


def pack(own, far, kv):
    places = lax.axis_size("y") * lax.axis_size("x")
    out = shape((places, own.shape[0], 2 * ROWS, PAY))
    return pl.pallas_call(
        pack_kernel,
        out_shape=out,
        compiler_params=params(6),
        cost_estimate=cost(0, 2 * out.size),
        name="pack_queries",
    )(own, far, kv)


def attend_kernel(plan_ref, q_ref, *refs):
    kv_refs, o_ref = refs[:KVH], refs[KVH]
    places = q_ref.shape[0]
    rows = places * 2 * ROWS
    y, x = lax.axis_index("y"), lax.axis_index("x")
    corner = (y - (y & 1)) * lax.axis_size("x") + x - (x & 1)
    near = [
        q_ref[corner + dy * lax.axis_size("x") + dx, 0, :, GW:].astype(F32)
        for dy in range(2)
        for dx in range(2)
    ]
    kb = jnp.concatenate([rows_of[:ROWS] for rows_of in near], axis=0).astype(BF16)
    vb = jnp.concatenate([rows_of[ROWS:] for rows_of in near], axis=0).astype(BF16)
    lane = lax.broadcasted_iota(jnp.int32, (rows, HD), 1)
    stats = jnp.zeros((rows, HD), F32)
    nt = (((1,), (1,)), ((), ()))
    for j in range(GRP):
        q = q_ref[:, 0, :, j * HD:(j + 1) * HD].reshape(rows, HD)
        parts = [
            lax.dot_general(q, kv_refs[x][0, :, :HD], nt, preferred_element_type=F32)
            for x in range(KVH)
        ]
        parts.append(lax.dot_general(q, kb, nt, preferred_element_type=F32))
        top = jnp.max(parts[0], axis=1, keepdims=True)
        for part in parts[1:]:
            top = jnp.maximum(top, jnp.max(part, axis=1, keepdims=True))
        total = jnp.zeros((rows, 1), F32)
        out = jnp.zeros((rows, HD), F32)
        for x, part in enumerate(parts):
            w = jnp.exp((part - top) * SCALE)
            total = total + jnp.sum(w, axis=1, keepdims=True)
            v = kv_refs[x][0, :, HD:] if x < KVH else vb
            out = out + jnp.dot(w.astype(BF16), v, preferred_element_type=F32)
        o_ref[:, 0, :, j * HD:(j + 1) * HD] = (
            (out * (1.0 / total)).astype(BF16).reshape(places, 2 * ROWS, HD)
        )
        for i, piece in enumerate(split_three(top * SCALE + jnp.log(total))):
            stats = jnp.where(lane == i * GRP + j, piece, stats)
    o_ref[:, 0, :, GW:] = stats.astype(BF16).reshape(places, 2 * ROWS, HD)


def attend(plan, queries, kv, first, units, member):
    places = queries.shape[0]
    dims = (places, 1, 2 * ROWS, PAY)
    keys = pl.BlockSpec((1,) + kv[0].shape[1:], lambda u, w: (member(u, w), 0, 0))
    pairs = units * places * 2 * ROWS * GRP * KVH * kv[0].shape[1]
    return pl.pallas_call(
        attend_kernel,
        grid_spec=pltpu.PrefetchScalarGridSpec(
            num_scalar_prefetch=1,
            grid=(units,),
            in_specs=[pl.BlockSpec(dims, lambda u, w: (0, first + u, 0, 0))] + [keys] * KVH,
            out_specs=pl.BlockSpec(dims, lambda u, w: (0, u, 0, 0)),
        ),
        out_shape=shape((places, units) + dims[2:]),
        compiler_params=params(24),
        cost_estimate=cost(pairs * HD * 4, 4 * queries.size + 8 * kv[0].size, pairs),
        name="attend",
    )(plan, queries, *kv)


def merge(members):
    top = members[0][1]
    for _, lse in members[1:]:
        top = jnp.maximum(top, lse)
    total = 0.0
    out = 0.0
    for part, lse in members:
        w = jnp.exp(lse - top)
        total = total + w
        out = out + part * w
    return out * (1.0 / total), top + jnp.log(total)


def fold_kernel(r_ref, own_ref, lse_ref, far_ref):
    units = r_ref.shape[1]
    rows = 2 * ROWS
    width = lax.axis_size("x")
    places = [
        [p for p in range(r_ref.shape[0]) if head_of(p // width, p % width) == h]
        for h in range(KVH)
    ]
    lane = lax.broadcasted_iota(jnp.int32, (rows, HD), 1)
    for u in range(units):
        near = jnp.zeros((rows, HD), F32)
        sent = jnp.zeros((rows, HD), F32)
        for x in range(KVH):
            tails = []
            for place in places[x]:
                tail = r_ref[place, u, :, GW:].astype(F32)
                tails.append(
                    tail[:, :GRP] + tail[:, GRP:2 * GRP] + tail[:, 2 * GRP:3 * GRP]
                )
            for j in range(GRP):
                h = x * GRP + j
                out, lse = merge([
                    (r_ref[place, u, :, j * HD:(j + 1) * HD].astype(F32), t[:, j:j + 1])
                    for place, t in zip(places[x], tails)
                ])
                own_ref[u, :, h * HD:(h + 1) * HD] = out[:ROWS]
                far_ref[u, :, h * HD:(h + 1) * HD] = out[ROWS:].astype(BF16)
                near = jnp.where(lane == h, lse, near)
                for i, piece in enumerate(split_three(lse)):
                    sent = jnp.where(lane == i * QH + h, piece, sent)
        lse_ref[u] = near[:ROWS]
        far_ref[u, :, QH * HD:] = sent[ROWS:].astype(BF16)


def fold(received):
    units = received.shape[1]
    return pl.pallas_call(
        fold_kernel,
        out_shape=(
            jax.ShapeDtypeStruct((units, ROWS, QH * HD), F32),
            jax.ShapeDtypeStruct((units, ROWS, HD), F32),
            jax.ShapeDtypeStruct((units, ROWS, QH * HD + HD), BF16),
        ),
        compiler_params=params(6),
        cost_estimate=cost(0, 4 * received.size),
        name="fold_plane",
    )(received)


def finish_kernel(sending, own_ref, lse_ref, far_ref, o_ref):
    half = QH // 2
    for u in range(own_ref.shape[0]):
        tail = far_ref[u, :, QH * HD:].astype(F32)
        far_lse = tail[:, :QH] + tail[:, QH:2 * QH] + tail[:, 2 * QH:3 * QH]
        for h in range(QH):
            cols = slice(h * HD, (h + 1) * HD)
            out, _ = merge([
                (own_ref[u, :, cols], lse_ref[u, :, h:h + 1]),
                (far_ref[u, :, cols].astype(F32), far_lse[:, h:h + 1]),
            ])
            out = out.astype(BF16)
            if sending:
                part = h % half
                for chip in range(o_ref.shape[0] // 2):
                    o_ref[2 * chip + h // half, :, part * HD:(part + 1) * HD] = out
            else:
                o_ref[u, :, cols] = out


def finish(own, lse, far, sending=False):
    out = shape(own.shape)
    if sending:
        out = shape((lax.axis_size("zl") * lax.axis_size("co"), ROWS, QH * HD // 2))
    return pl.pallas_call(
        functools.partial(finish_kernel, sending),
        out_shape=out,
        compiler_params=params(4),
        cost_estimate=cost(0, 8 * own.size),
        name="finish",
    )(own, lse, far)


def swap(value, axis):
    return lax.ppermute(value, axis, [(0, 1), (1, 0)])


def exchange(value, axes):
    return lax.all_to_all(value, axes, split_axis=0, concat_axis=0, tiled=True)


def across(value, d):
    width = lax.axis_size("x")
    steps = (d & 1) + width * (d >> 1)
    return lax.ppermute(value, PLANE, [(i, i ^ steps) for i in range(width * lax.axis_size("y"))])


def after(value, *earlier):
    return lax.optimization_barrier((value,) + earlier)[0]


def masked_rows(values, masked, filler):
    return jnp.where(masked[..., None] == 1, filler, values)


def body(
    stored_memory,
    opening_probe_vectors,
    opening_memory_pairs,
    opening_hidden_marks,
    second_probe_vectors,
    second_memory_pairs,
    second_hidden_marks,
    continuing_sequence_ids,
    blank_symbol_probe,
    blank_symbol_pairs,
):
    seqs = stored_memory.shape[0]
    wide, pair = QH * HD, 2 * KVH * HD
    plan = make_plan(continuing_sequence_ids, seqs)
    slot_halves = exchange(
        send_slots(
            second_probe_vectors,
            second_memory_pairs,
            second_hidden_marks,
            blank_symbol_probe,
            blank_symbol_pairs,
        ),
        DP,
    )
    pieces = cut_by_head(stored_memory)
    kv = [pieces[0]] + [across(piece, d) for d, piece in enumerate(pieces) if d]

    query_first = masked_rows(opening_probe_vectors, opening_hidden_marks, blank_symbol_probe)
    block_first = masked_rows(opening_memory_pairs, opening_hidden_marks, blank_symbol_pairs)

    homes = continuing_sequence_ids // seqs
    slots = jnp.arange(homes.shape[0], dtype=jnp.int32)
    earlier = (homes[None, :] == homes[:, None]) & (slots[None, :] < slots[:, None])
    waits = jnp.any(earlier, axis=1)

    def second_queries(turn, halves, *aheads):
        got = swap(pick(plan, halves, OTHER + turn), "co")
        return join(plan, halves, got, SLOT + turn, (wide, pair), *aheads)

    def second_member(turn):
        return lambda unit, plan_ref: plan_ref[MEMBER + turn]

    def hand_back(home_halves):
        back = exchange(home_halves, DP)
        got = swap(pick(plan, back, HOME_OTHER), "co")
        return join(plan, back, got, HOME, (wide,))[0]

    def last_pass(early):
        queries, pairs = second_queries(1, slot_halves)
        second_in = exchange(pack(queries, swap(queries, "zh"), pairs), PLANE)
        second_part = attend(plan, second_in, kv, 0, 1, second_member(1))
        own, lse, far = fold(exchange(second_part, PLANE))
        late = hand_back(finish(own, lse, swap(far, "zh"), True))
        group = lax.axis_index("zl") * lax.axis_size("co") + lax.axis_index("co")
        return jnp.where(waits[group], late, early)

    queries, pairs = second_queries(
        0, after(slot_halves, kv[1], kv[2]), query_first, block_first
    )
    far = swap(queries, "zh")
    everything = exchange(pack(queries, after(far, kv[3]), pairs), PLANE)
    second_part = attend(plan, everything, kv, seqs, 1, second_member(0))
    first_part = attend(plan, everything, kv, 0, seqs, lambda unit, plan_ref: unit)
    second_back = exchange(second_part, PLANE)
    first_back = exchange(after(first_part, second_back), PLANE)
    own, lse, far = fold(second_back)
    home_out = finish(own, lse, swap(far, "zh"), True)
    own_first, lse_first, far_first = fold(first_back)
    result = hand_back(after(home_out, first_back))
    first_out = finish(own_first, lse_first, swap(far_first, "zh"))
    result = lax.cond(jnp.any(waits), last_pass, lambda early: early, result)
    return first_out, result


def solution(mesh):
    fine = Mesh(mesh.devices.reshape(8, 2, 2, 4, 4), ("zl", "co", "zh", "y", "x"))
    rows = P(DP, CTX, None)
    marks = P(DP, CTX)
    return jax.shard_map(
        body,
        mesh=fine,
        in_specs=(rows, rows, rows, marks, rows, rows, marks, P(), P(), P()),
        out_specs=(rows, rows),
        check_vma=False,
    )
```

```python
import functools

import jax
import jax.numpy as jnp
from jax import lax
from jax.experimental import pallas as pl
from jax.experimental.pallas import tpu as pltpu
from jax.sharding import Mesh, PartitionSpec as P

QH = 16
KVH = 4
HD = 128
GRP = QH // KVH
GW = GRP * HD
ROWS = 8
PAY = GW + HD
DP = ("zl", "co")
PLANE = ("y", "x")
CTX = ("zh", "y", "x")
SCALE = HD ** -0.5
LOG2E = 1.4426950408889634
F32 = jnp.float32
BF16 = jnp.bfloat16


def cost(flops, nbytes, trans=0):
    return pl.CostEstimate(flops=flops, bytes_accessed=nbytes, transcendentals=trans)


def params(mib):
    return pltpu.CompilerParams(vmem_limit_bytes=mib * 2 ** 20)


def shape(dims, dtype=BF16):
    return jax.ShapeDtypeStruct(dims, dtype)


def in_smem():
    return pl.BlockSpec(memory_space=pltpu.SMEM)


def in_vmem():
    return pl.BlockSpec(memory_space=pltpu.VMEM)


def split_three(v):
    hi = v.astype(BF16)
    rest = v - hi.astype(F32)
    mid = rest.astype(BF16)
    low = (rest - mid.astype(F32)).astype(BF16)
    return hi.astype(F32), mid.astype(F32), low.astype(F32)


SLOT, OTHER, MEMBER, HOME, HOME_OTHER, SHARED, WAITS = 0, 2, 4, 6, 7, 8, 9


def plan_kernel(seqs, ids_ref, o_ref):
    count = ids_ref.shape[0]
    core = lax.axis_index("co")
    group = lax.axis_index("zl") * lax.axis_size("co") + core
    other = group + 1 - 2 * core
    for where, place in ((group, SLOT), (other, OTHER)):
        seen = jnp.int32(0)
        slot = [jnp.int32(0), jnp.int32(0)]
        member = [jnp.int32(0), jnp.int32(0)]
        for j in range(count):
            one = ids_ref[j]
            home = lax.div(one, jnp.int32(seqs))
            hit = home == where
            for turn in range(2):
                now = hit & (seen == turn)
                slot[turn] = jnp.where(now, j, slot[turn])
                member[turn] = jnp.where(now, one - home * seqs, member[turn])
            seen = seen + hit.astype(jnp.int32)
        for turn in range(2):
            o_ref[place + turn] = slot[turn]
            if place == SLOT:
                o_ref[MEMBER + turn] = member[turn]
    taken, shared, waits = jnp.int32(0), jnp.int32(0), jnp.int32(0)
    for j in range(count):
        bit = lax.shift_left(jnp.int32(1), lax.div(ids_ref[j], jnp.int32(seqs)))
        second = ((taken & bit) != 0).astype(jnp.int32)
        shared = shared | second
        waits = jnp.where(group == j, second, waits)
        taken = taken | bit
    o_ref[SHARED] = shared
    o_ref[WAITS] = waits
    o_ref[HOME] = lax.div(ids_ref[group], jnp.int32(seqs))
    o_ref[HOME_OTHER] = lax.div(ids_ref[other], jnp.int32(seqs))


def make_plan(ids, seqs):
    return pl.pallas_call(
        functools.partial(plan_kernel, seqs),
        in_specs=[in_smem()],
        out_specs=in_smem(),
        out_shape=shape((10,), jnp.int32),
        compiler_params=params(1),
        cost_estimate=cost(0, 128),
        name="plan",
    )(ids)


def head_of(y, x):
    return 2 * (y & 1) + (x & 1)


def own_head():
    return head_of(lax.axis_index("y"), lax.axis_index("x"))


def cut_kernel(s_ref, *outs):
    here = own_head()
    for d, out in enumerate(outs):
        head = jnp.bitwise_xor(here, d)
        for part in range(2):
            start = pl.multiple_of((part * KVH + head) * HD, HD)
            for n in range(out.shape[0]):
                out[n, :, part * HD:(part + 1) * HD] = s_ref[n, :, pl.ds(start, HD)]


def cut_by_head(stored):
    seqs, rows, _ = stored.shape
    return pl.pallas_call(
        cut_kernel,
        out_shape=[shape((seqs, rows, 2 * HD))] * KVH,
        compiler_params=params(12),
        cost_estimate=cost(0, 4 * stored.size),
        name="cut_by_head",
    )(stored)


def send_kernel(*refs):
    given, o_ref, held, sem = refs[:5], refs[5], refs[6:11], refs[11]
    copies = [pltpu.make_async_copy(a, b, sem.at[n]) for n, (a, b) in enumerate(zip(given, held))]
    for copy in copies:
        copy.start()
    for copy in copies:
        copy.wait()
    q_ref, kv_ref, mark_ref, bq_ref, bkv_ref = held
    square = (ROWS, ROWS)
    eye = lax.broadcasted_iota(jnp.int32, square, 0) == lax.broadcasted_iota(jnp.int32, square, 1)
    marks = jnp.broadcast_to(mark_ref[...], square)
    column = jnp.sum(jnp.where(eye, marks, 0).astype(F32), axis=1, keepdims=True)
    hidden = jnp.broadcast_to(column == 1.0, (ROWS, HD))
    for blank, values, first in ((bq_ref, q_ref, 0), (bkv_ref, kv_ref, q_ref.shape[2] // 2)):
        half = values.shape[2] // 2
        for c in range(2):
            value = jnp.concatenate(
                [
                    jnp.where(
                        hidden,
                        jnp.broadcast_to(blank[i:i + 1].astype(F32), (ROWS, HD)),
                        values[0, :, i * HD:(i + 1) * HD].astype(F32),
                    )
                    for i in range(c * half // HD, (c + 1) * half // HD)
                ],
                axis=1,
            ).astype(BF16)
            for chip in range(o_ref.shape[0] // 2):
                o_ref[2 * chip + c, :, first:first + half] = value


def send_slots(q, kv, marks, blank_q, blank_kv):
    groups = lax.axis_size("zl") * lax.axis_size("co")
    out = shape((groups, ROWS, (q.shape[2] + kv.shape[2]) // 2))
    given = (q, kv, marks, blank_q.reshape(-1, HD), blank_kv.reshape(-1, HD))
    return pl.pallas_call(
        send_kernel,
        in_specs=[pl.BlockSpec(memory_space=pltpu.HBM)] * len(given),
        out_specs=in_vmem(),
        out_shape=out,
        scratch_shapes=[pltpu.VMEM(value.shape, value.dtype) for value in given]
        + [pltpu.SemaphoreType.DMA((len(given),))],
        cost_estimate=cost(0, 2 * out.size),
        name="send_slots",
    )(*given)


def pick_kernel(entries, plan_ref, halves_ref, *outs):
    for entry, out in zip(entries, outs):
        out[0] = halves_ref[plan_ref[entry]]


def pick(plan, halves, entries):
    return pl.pallas_call(
        functools.partial(pick_kernel, entries),
        in_specs=[in_smem(), in_vmem()],
        out_specs=[in_vmem()] * len(entries),
        out_shape=[shape((1,) + halves.shape[1:])] * len(entries),
        compiler_params=params(2),
        cost_estimate=cost(0, 4 * halves.size),
        name="pick",
    )(plan, halves)


def join_kernel(given, kept_ref, got_ref, *refs):
    aheads, outs = refs[:given], refs[given:]
    low = lax.axis_index("co") == 0
    first = 0
    for n, out in enumerate(outs):
        last = out.shape[0] - 1
        if given:
            out[:last] = aheads[n][...]
        half = out.shape[2] // 2
        cols = slice(first, first + half)

        @pl.when(low)
        def _(out=out, last=last, half=half, cols=cols):
            out[last, :, :half] = kept_ref[0, :, cols]
            out[last, :, half:] = got_ref[0, :, cols]

        @pl.when(jnp.logical_not(low))
        def _(out=out, last=last, half=half, cols=cols):
            out[last, :, :half] = got_ref[0, :, cols]
            out[last, :, half:] = kept_ref[0, :, cols]

        first += half


def join(kept, got, widths, *aheads):
    units = 1 + (aheads[0].shape[0] if aheads else 0)
    return pl.pallas_call(
        functools.partial(join_kernel, len(aheads)),
        out_shape=[shape((units, ROWS, width)) for width in widths],
        compiler_params=params(2),
        cost_estimate=cost(0, 8 * kept.size),
        name="join",
    )(kept, got, *aheads)


def pack_kernel(own_ref, far_ref, kv_ref, o_ref):
    width = lax.axis_size("x")
    for u in range(own_ref.shape[0]):
        for h in range(KVH):
            cols = slice(h * GW, (h + 1) * GW)
            q = jnp.concatenate(
                [own_ref[u, :, cols].astype(F32), far_ref[u, :, cols].astype(F32)], axis=0
            ).astype(BF16)
            k = kv_ref[u, :, h * HD:(h + 1) * HD].astype(F32)
            v = kv_ref[u, :, (KVH + h) * HD:(KVH + h + 1) * HD].astype(F32)
            kv = jnp.concatenate([k, v], axis=0).astype(BF16)
            for place in range(o_ref.shape[0]):
                if head_of(place // width, place % width) == h:
                    o_ref[place, u, :, :GW] = q
                    o_ref[place, u, :, GW:] = kv


def pack(own, far, kv):
    places = lax.axis_size("y") * lax.axis_size("x")
    out = shape((places, own.shape[0], 2 * ROWS, PAY))
    return pl.pallas_call(
        pack_kernel,
        out_shape=out,
        compiler_params=params(6),
        cost_estimate=cost(0, 2 * out.size),
        name="pack_queries",
    )(own, far, kv)


def attend_kernel(first, members, plan_ref, q_ref, *refs):
    kv_refs, o_ref, k_all, v_all = refs[:KVH], refs[KVH], refs[KVH + 1], refs[KVH + 2]
    places, units = o_ref.shape[:2]
    rows = places * 2 * ROWS
    span = kv_refs[0].shape[1]
    cached = KVH * span
    y, x = lax.axis_index("y"), lax.axis_index("x")
    width = lax.axis_size("x")
    corner = (y - (y & 1)) * width + x - (x & 1)
    lane = lax.broadcasted_iota(jnp.int32, (rows, HD), 1)
    v_all[:, HD:] = jnp.ones((cached + KVH * ROWS, HD), BF16)
    for u in range(units):
        member = members[u](plan_ref)
        for n, kv_ref in enumerate(kv_refs):
            k_all[n * span:(n + 1) * span] = kv_ref[member, :, :HD]
            v_all[n * span:(n + 1) * span, :HD] = kv_ref[member, :, HD:]
        near = [
            q_ref[corner + dy * width + dx, first + u, :, GW:].astype(F32)
            for dy in range(2)
            for dx in range(2)
        ]
        k_all[cached:] = jnp.concatenate([part[:ROWS] for part in near], axis=0).astype(BF16)
        v_all[cached:, :HD] = jnp.concatenate([part[ROWS:] for part in near], axis=0).astype(BF16)
        stats = jnp.zeros((rows, HD), F32)
        for j in range(GRP):
            cols = slice(j * HD, (j + 1) * HD)
            q = q_ref[:, first + u, :, cols].reshape(rows, HD)
            scores = lax.dot_general(
                q, k_all[...], (((1,), (1,)), ((), ())), preferred_element_type=F32
            )
            top = jnp.max(scores, axis=1, keepdims=True)
            w = jnp.exp2((scores - top) * (SCALE * LOG2E))
            both = jnp.dot(w.astype(BF16), v_all[...], preferred_element_type=F32)
            total = both[:, HD:]
            out = both[:, :HD] * (1.0 / total)
            o_ref[:, u, :, cols] = out.astype(BF16).reshape(places, 2 * ROWS, HD)
            for i, piece in enumerate(split_three(top * SCALE + jnp.log(total))):
                stats = jnp.where(lane == i * GRP + j, piece, stats)
        o_ref[:, u, :, GW:] = stats.astype(BF16).reshape(places, 2 * ROWS, HD)


def attend(plan, queries, kv, first, members):
    places, units = queries.shape[0], len(members)
    keys = KVH * (kv[0].shape[1] + ROWS)
    pairs = units * places * 2 * ROWS * GRP * keys
    return pl.pallas_call(
        functools.partial(attend_kernel, first, members),
        in_specs=[in_smem()] + [in_vmem()] * (1 + KVH),
        out_specs=in_vmem(),
        out_shape=shape((places, units) + queries.shape[2:]),
        scratch_shapes=[pltpu.VMEM((keys, HD), BF16), pltpu.VMEM((keys, 2 * HD), BF16)],
        compiler_params=params(20),
        cost_estimate=cost(pairs * HD * 4, 4 * queries.size + 8 * kv[0].size, pairs),
        name="attend",
    )(plan, queries, *kv)


def merge(members):
    top = members[0][1]
    for _, lse in members[1:]:
        top = jnp.maximum(top, lse)
    total = 0.0
    out = 0.0
    for part, lse in members:
        w = jnp.exp(lse - top)
        total = total + w
        out = out + part * w
    return out * (1.0 / total), top + jnp.log(total)


def fold_kernel(r_ref, own_ref, lse_ref, far_ref):
    units = r_ref.shape[1]
    rows = 2 * ROWS
    width = lax.axis_size("x")
    places = [
        [p for p in range(r_ref.shape[0]) if head_of(p // width, p % width) == h]
        for h in range(KVH)
    ]
    lane = lax.broadcasted_iota(jnp.int32, (rows, HD), 1)
    for u in range(units):
        near = jnp.zeros((rows, HD), F32)
        sent = jnp.zeros((rows, HD), F32)
        for x in range(KVH):
            tails = []
            for place in places[x]:
                tail = r_ref[place, u, :, GW:].astype(F32)
                tails.append(
                    tail[:, :GRP] + tail[:, GRP:2 * GRP] + tail[:, 2 * GRP:3 * GRP]
                )
            for j in range(GRP):
                h = x * GRP + j
                out, lse = merge([
                    (r_ref[place, u, :, j * HD:(j + 1) * HD].astype(F32), t[:, j:j + 1])
                    for place, t in zip(places[x], tails)
                ])
                own_ref[u, :, h * HD:(h + 1) * HD] = out[:ROWS]
                far_ref[u, :, h * HD:(h + 1) * HD] = out[ROWS:].astype(BF16)
                near = jnp.where(lane == h, lse, near)
                for i, piece in enumerate(split_three(lse)):
                    sent = jnp.where(lane == i * QH + h, piece, sent)
        lse_ref[u] = near[:ROWS]
        far_ref[u, :, QH * HD:] = sent[ROWS:].astype(BF16)


def fold(received):
    units = received.shape[1]
    return pl.pallas_call(
        fold_kernel,
        out_shape=(
            jax.ShapeDtypeStruct((units, ROWS, QH * HD), F32),
            jax.ShapeDtypeStruct((units, ROWS, HD), F32),
            jax.ShapeDtypeStruct((units, ROWS, QH * HD + HD), BF16),
        ),
        compiler_params=params(6),
        cost_estimate=cost(0, 4 * received.size),
        name="fold_plane",
    )(received)


def finish_kernel(sending, own_ref, lse_ref, far_ref, o_ref):
    half = QH // 2
    for u in range(own_ref.shape[0]):
        tail = far_ref[u, :, QH * HD:].astype(F32)
        far_lse = tail[:, :QH] + tail[:, QH:2 * QH] + tail[:, 2 * QH:3 * QH]
        for h in range(QH):
            cols = slice(h * HD, (h + 1) * HD)
            out, _ = merge([
                (own_ref[u, :, cols], lse_ref[u, :, h:h + 1]),
                (far_ref[u, :, cols].astype(F32), far_lse[:, h:h + 1]),
            ])
            out = out.astype(BF16)
            if sending:
                part = h % half
                for chip in range(o_ref.shape[0] // 2):
                    o_ref[2 * chip + h // half, :, part * HD:(part + 1) * HD] = out
            else:
                o_ref[u, :, cols] = out


def finish(own, lse, far, sending=False):
    out = shape(own.shape)
    if sending:
        out = shape((lax.axis_size("zl") * lax.axis_size("co"), ROWS, QH * HD // 2))
    return pl.pallas_call(
        functools.partial(finish_kernel, sending),
        out_shape=out,
        compiler_params=params(4),
        cost_estimate=cost(0, 8 * own.size),
        name="finish",
    )(own, lse, far)


def swap(value, axis):
    return lax.ppermute(value, axis, [(0, 1), (1, 0)])


def exchange(value, axes):
    return lax.all_to_all(value, axes, split_axis=0, concat_axis=0, tiled=True)


def across(value, d):
    width = lax.axis_size("x")
    steps = (d & 1) + width * (d >> 1)
    return lax.ppermute(value, PLANE, [(i, i ^ steps) for i in range(width * lax.axis_size("y"))])


def after(value, *earlier):
    return lax.optimization_barrier((value,) + earlier)[0]


def masked_rows(values, masked, filler):
    return jnp.where(masked[..., None] == 1, filler, values)


def body(
    stored_memory,
    opening_probe_vectors,
    opening_memory_pairs,
    opening_hidden_marks,
    second_probe_vectors,
    second_memory_pairs,
    second_hidden_marks,
    continuing_sequence_ids,
    blank_symbol_probe,
    blank_symbol_pairs,
):
    seqs = stored_memory.shape[0]
    wide, pair = QH * HD, 2 * KVH * HD
    plan = make_plan(continuing_sequence_ids, seqs)
    slot_halves = exchange(
        send_slots(
            second_probe_vectors,
            second_memory_pairs,
            second_hidden_marks,
            blank_symbol_probe,
            blank_symbol_pairs,
        ),
        DP,
    )
    pieces = cut_by_head(stored_memory)
    kv = [pieces[0]] + [across(piece, d) for d, piece in enumerate(pieces) if d]

    query_first = masked_rows(opening_probe_vectors, opening_hidden_marks, blank_symbol_probe)
    block_first = masked_rows(opening_memory_pairs, opening_hidden_marks, blank_symbol_pairs)

    def second_queries(turn, *aheads):
        kept, lent = pick(plan, slot_halves, (SLOT + turn, OTHER + turn))
        return join(kept, swap(lent, "co"), (wide, pair), *aheads)

    def second_member(turn):
        return lambda plan_ref: plan_ref[MEMBER + turn]

    def hand_back(home_halves, *earlier):
        back = after(exchange(home_halves, DP), *earlier)
        kept, lent = pick(plan, back, (HOME, HOME_OTHER))
        return kept, swap(lent, "co")

    def last_pass(early):
        queries, pairs = second_queries(1)
        second_in = exchange(pack(queries, swap(queries, "zh"), pairs), PLANE)
        second_part = attend(plan, second_in, kv, 0, [second_member(1)])
        own, lse, far = fold(exchange(second_part, PLANE))
        late = hand_back(finish(own, lse, swap(far, "zh"), True))
        return tuple(jnp.where(plan[WAITS] > 0, new, old) for new, old in zip(late, early))

    queries, pairs = second_queries(0, query_first, block_first)
    far = swap(queries, "zh")
    everything = exchange(pack(queries, after(far, *kv[1:]), pairs), PLANE)

    second_part = attend(plan, everything, kv, seqs, [second_member(0)])
    first_part = attend(plan, everything, kv, 0, [lambda plan_ref, n=n: n for n in range(seqs)])
    second_back = exchange(second_part, PLANE)
    first_back = exchange(after(first_part, second_back), PLANE)
    own, lse, far = fold(second_back)
    home_out = finish(own, lse, swap(far, "zh"), True)
    own_first, lse_first, far_first = fold(first_back)
    first_out = finish(own_first, lse_first, swap(far_first, "zh"))
    shared = plan[SHARED] > 0
    halves = hand_back(after(home_out, first_back), first_out, shared)
    halves = lax.cond(shared, last_pass, lambda early: early, halves)
    return first_out, join(*halves, (wide,))[0]


def solution(mesh):
    fine = Mesh(mesh.devices.reshape(8, 2, 2, 4, 4), ("zl", "co", "zh", "y", "x"))
    rows = P(DP, CTX, None)
    marks = P(DP, CTX)
    return jax.shard_map(
        body,
        mesh=fine,
        in_specs=(rows, rows, rows, marks, rows, rows, marks, P(), P(), P()),
        out_specs=(rows, rows),
        check_vma=False,
    )
```

```python
import functools

import jax
import jax.numpy as jnp
from jax import lax
from jax.experimental import pallas as pl
from jax.experimental.pallas import tpu as pltpu
from jax.sharding import Mesh, PartitionSpec as P

QH = 16
KVH = 4
HD = 128
GRP = QH // KVH
GW = GRP * HD
ROWS = 8
DP = ("zl", "co")
PLANE = ("y", "x")
CTX = ("zh", "y", "x")
SCALE = HD ** -0.5
LOG2E = 1.4426950408889634
F32 = jnp.float32
BF16 = jnp.bfloat16


def cost(flops, nbytes, trans=0):
    return pl.CostEstimate(flops=flops, bytes_accessed=nbytes, transcendentals=trans)


def params(mib):
    return pltpu.CompilerParams(vmem_limit_bytes=mib * 2 ** 20)


def shape(dims, dtype=BF16):
    return jax.ShapeDtypeStruct(dims, dtype)


def in_smem():
    return pl.BlockSpec(memory_space=pltpu.SMEM)


def in_vmem():
    return pl.BlockSpec(memory_space=pltpu.VMEM)


def split_three(v):
    hi = v.astype(BF16)
    rest = v - hi.astype(F32)
    mid = rest.astype(BF16)
    low = (rest - mid.astype(F32)).astype(BF16)
    return hi.astype(F32), mid.astype(F32), low.astype(F32)


SLOT, OTHER, MEMBER, HOME, HOME_OTHER, SHARED, WAITS = 0, 2, 4, 6, 7, 8, 9


def plan_kernel(seqs, ids_ref, o_ref):
    count = ids_ref.shape[0]
    core = lax.axis_index("co")
    group = lax.axis_index("zl") * lax.axis_size("co") + core
    other = group + 1 - 2 * core
    for where, place in ((group, SLOT), (other, OTHER)):
        seen = jnp.int32(0)
        slot = [jnp.int32(0), jnp.int32(0)]
        member = [jnp.int32(0), jnp.int32(0)]
        for j in range(count):
            one = ids_ref[j]
            home = lax.div(one, jnp.int32(seqs))
            hit = home == where
            for turn in range(2):
                now = hit & (seen == turn)
                slot[turn] = jnp.where(now, j, slot[turn])
                member[turn] = jnp.where(now, one - home * seqs, member[turn])
            seen = seen + hit.astype(jnp.int32)
        for turn in range(2):
            o_ref[place + turn] = slot[turn]
            if place == SLOT:
                o_ref[MEMBER + turn] = member[turn]
    taken, shared, waits = jnp.int32(0), jnp.int32(0), jnp.int32(0)
    for j in range(count):
        bit = lax.shift_left(jnp.int32(1), lax.div(ids_ref[j], jnp.int32(seqs)))
        second = ((taken & bit) != 0).astype(jnp.int32)
        shared = shared | second
        waits = jnp.where(group == j, second, waits)
        taken = taken | bit
    o_ref[SHARED] = shared
    o_ref[WAITS] = waits
    o_ref[HOME] = lax.div(ids_ref[group], jnp.int32(seqs))
    o_ref[HOME_OTHER] = lax.div(ids_ref[other], jnp.int32(seqs))


def make_plan(ids, seqs):
    return pl.pallas_call(
        functools.partial(plan_kernel, seqs),
        in_specs=[in_smem()],
        out_specs=in_smem(),
        out_shape=shape((10,), jnp.int32),
        compiler_params=params(1),
        cost_estimate=cost(0, 128),
        name="plan",
    )(ids)


def head_of(y, x):
    return 2 * (y & 1) + (x & 1)


def own_head():
    return head_of(lax.axis_index("y"), lax.axis_index("x"))


def cut_kernel(s_ref, b_ref, *outs):
    here = own_head()
    seqs, rows, _ = s_ref.shape
    for d, out in enumerate(outs):
        head = jnp.bitwise_xor(here, d)
        for part in range(2):
            columns = pl.ds(pl.multiple_of((part * KVH + head) * HD, HD), HD)
            cols = slice(part * HD, (part + 1) * HD)
            for n in range(seqs):
                out[n * rows:(n + 1) * rows, cols] = s_ref[n, :, columns]
            blocks = [b_ref[n, :, columns].astype(F32) for n in range(seqs)]
            out[seqs * rows:, cols] = jnp.concatenate(blocks, axis=0).astype(BF16)


def cut_by_head(stored, blocks):
    seqs, rows, _ = stored.shape
    return pl.pallas_call(
        cut_kernel,
        out_shape=[shape((seqs * (rows + ROWS), 2 * HD))] * KVH,
        compiler_params=params(12),
        cost_estimate=cost(0, 4 * stored.size),
        name="cut_by_head",
    )(stored, blocks)


def send_kernel(*refs):
    given, o_ref, held, sem = refs[:5], refs[5], refs[6:11], refs[11]
    copies = [pltpu.make_async_copy(a, b, sem.at[n]) for n, (a, b) in enumerate(zip(given, held))]
    for copy in copies:
        copy.start()
    for copy in copies:
        copy.wait()
    q_ref, kv_ref, mark_ref, bq_ref, bkv_ref = held
    square = (ROWS, ROWS)
    eye = lax.broadcasted_iota(jnp.int32, square, 0) == lax.broadcasted_iota(jnp.int32, square, 1)
    marks = jnp.broadcast_to(mark_ref[...], square)
    column = jnp.sum(jnp.where(eye, marks, 0).astype(F32), axis=1, keepdims=True)
    hidden = jnp.broadcast_to(column == 1.0, (ROWS, HD))
    for blank, values, first in ((bq_ref, q_ref, 0), (bkv_ref, kv_ref, q_ref.shape[2] // 2)):
        half = values.shape[2] // 2
        for c in range(2):
            value = jnp.concatenate(
                [
                    jnp.where(
                        hidden,
                        jnp.broadcast_to(blank[i:i + 1].astype(F32), (ROWS, HD)),
                        values[0, :, i * HD:(i + 1) * HD].astype(F32),
                    )
                    for i in range(c * half // HD, (c + 1) * half // HD)
                ],
                axis=1,
            ).astype(BF16)
            for chip in range(o_ref.shape[0] // 2):
                o_ref[2 * chip + c, :, first:first + half] = value


def send_slots(q, kv, marks, blank_q, blank_kv):
    groups = lax.axis_size("zl") * lax.axis_size("co")
    out = shape((groups, ROWS, (q.shape[2] + kv.shape[2]) // 2))
    given = (q, kv, marks, blank_q.reshape(-1, HD), blank_kv.reshape(-1, HD))
    return pl.pallas_call(
        send_kernel,
        in_specs=[pl.BlockSpec(memory_space=pltpu.HBM)] * len(given),
        out_specs=in_vmem(),
        out_shape=out,
        scratch_shapes=[pltpu.VMEM(value.shape, value.dtype) for value in given]
        + [pltpu.SemaphoreType.DMA((len(given),))],
        cost_estimate=cost(0, 2 * out.size),
        name="send_slots",
    )(*given)


def pick_kernel(entries, plan_ref, halves_ref, *outs):
    for entry, out in zip(entries, outs):
        out[0] = halves_ref[plan_ref[entry]]


def pick(plan, halves, entries):
    return pl.pallas_call(
        functools.partial(pick_kernel, entries),
        in_specs=[in_smem(), in_vmem()],
        out_specs=[in_vmem()] * len(entries),
        out_shape=[shape((1,) + halves.shape[1:])] * len(entries),
        compiler_params=params(2),
        cost_estimate=cost(0, 4 * halves.size),
        name="pick",
    )(plan, halves)


def join_kernel(given, kept_ref, got_ref, *refs):
    aheads, outs = refs[:given], refs[given:]
    low = lax.axis_index("co") == 0
    first = 0
    for n, out in enumerate(outs):
        last = out.shape[0] - 1
        if n < given:
            out[:last] = aheads[n][...]
        half = out.shape[2] // 2
        cols = slice(first, first + half)

        @pl.when(low)
        def _(out=out, last=last, half=half, cols=cols):
            out[last, :, :half] = kept_ref[0, :, cols]
            out[last, :, half:] = got_ref[0, :, cols]

        @pl.when(jnp.logical_not(low))
        def _(out=out, last=last, half=half, cols=cols):
            out[last, :, :half] = got_ref[0, :, cols]
            out[last, :, half:] = kept_ref[0, :, cols]

        first += half


def join(kept, got, widths, *aheads):
    ahead = [value.shape[0] for value in aheads] + [0] * (len(widths) - len(aheads))
    return pl.pallas_call(
        functools.partial(join_kernel, len(aheads)),
        out_shape=[shape((units + 1, ROWS, width)) for units, width in zip(ahead, widths)],
        compiler_params=params(2),
        cost_estimate=cost(0, 8 * kept.size),
        name="join",
    )(kept, got, *aheads)


def pack_kernel(own_ref, far_ref, kv_ref, o_ref):
    width = lax.axis_size("x")
    units = own_ref.shape[0]
    for h in range(KVH):
        cols = slice(h * GW, (h + 1) * GW)
        values = [
            jnp.concatenate(
                [own_ref[u, :, cols].astype(F32), far_ref[u, :, cols].astype(F32)], axis=0
            ).astype(BF16)
            for u in range(units)
        ]
        k = kv_ref[0, :, h * HD:(h + 1) * HD].astype(F32)
        v = kv_ref[0, :, (KVH + h) * HD:(KVH + h + 1) * HD].astype(F32)
        kv = jnp.concatenate([k, v], axis=0).astype(BF16)
        for place in range(o_ref.shape[0]):
            if head_of(place // width, place % width) == h:
                for u, value in enumerate(values):
                    o_ref[place, :, u * GW:(u + 1) * GW] = value
                o_ref[place, :, units * GW:] = kv


def pack(own, far, kv):
    places = lax.axis_size("y") * lax.axis_size("x")
    out = shape((places, 2 * ROWS, own.shape[0] * GW + HD))
    return pl.pallas_call(
        pack_kernel,
        out_shape=out,
        compiler_params=params(6),
        cost_estimate=cost(0, 2 * out.size),
        name="pack_queries",
    )(own, far, kv)


def attend_kernel(members, seqs, plan_ref, q_ref, *refs):
    kv_refs, o_ref, k_all, v_all = refs[:KVH], refs[KVH], refs[KVH + 1], refs[KVH + 2]
    places, units = o_ref.shape[0], len(members)
    rows = places * 2 * ROWS
    span = kv_refs[0].shape[0] // seqs - ROWS
    cached = KVH * span
    y, x = lax.axis_index("y"), lax.axis_index("x")
    width = lax.axis_size("x")
    corner = (y - (y & 1)) * width + x - (x & 1)
    lane = lax.broadcasted_iota(jnp.int32, (rows, HD), 1)
    stats = jnp.zeros((rows, HD), F32)
    v_all[:, HD:] = jnp.ones((cached + KVH * ROWS, HD), BF16)
    for u, member in enumerate(members):
        if isinstance(member, int):
            blocks = [kv_ref[seqs * span:].astype(F32) for kv_ref in kv_refs]
            own = slice(member * ROWS, (member + 1) * ROWS)
            near = [(block[own, :HD], block[own, HD:]) for block in blocks]
            start = member * span
        else:
            blocks = [
                q_ref[corner + dy * width + dx, :, units * GW:].astype(F32)
                for dy in range(2)
                for dx in range(2)
            ]
            near = [(block[:ROWS], block[ROWS:]) for block in blocks]
            start = pl.multiple_of(member(plan_ref) * span, span)
        for n, kv_ref in enumerate(kv_refs):
            k_all[n * span:(n + 1) * span] = kv_ref[pl.ds(start, span), :HD]
            v_all[n * span:(n + 1) * span, :HD] = kv_ref[pl.ds(start, span), HD:]
        k_all[cached:] = jnp.concatenate([k for k, _ in near], axis=0).astype(BF16)
        v_all[cached:, :HD] = jnp.concatenate([v for _, v in near], axis=0).astype(BF16)
        for j in range(GRP):
            cols = slice(u * GW + j * HD, u * GW + (j + 1) * HD)
            q = q_ref[:, :, cols].reshape(rows, HD)
            scores = lax.dot_general(
                q, k_all[...], (((1,), (1,)), ((), ())), preferred_element_type=F32
            )
            top = jnp.max(scores, axis=1, keepdims=True)
            w = jnp.exp2((scores - top) * (SCALE * LOG2E))
            both = jnp.dot(w.astype(BF16), v_all[...], preferred_element_type=F32)
            total = both[:, HD:]
            out = both[:, :HD] * (1.0 / total)
            o_ref[:, :, cols] = out.astype(BF16).reshape(places, 2 * ROWS, HD)
            for i, piece in enumerate(split_three(top * SCALE + jnp.log(total))):
                stats = jnp.where(lane == (3 * u + i) * GRP + j, piece, stats)
    o_ref[:, :, units * GW:] = stats.astype(BF16).reshape(places, 2 * ROWS, HD)


def attend(plan, queries, kv, members, seqs):
    places, units = queries.shape[0], len(members)
    keys = KVH * (kv[0].shape[0] // seqs)
    pairs = units * places * 2 * ROWS * GRP * keys
    return pl.pallas_call(
        functools.partial(attend_kernel, members, seqs),
        in_specs=[in_smem()] + [in_vmem()] * (1 + KVH),
        out_specs=in_vmem(),
        out_shape=shape(queries.shape),
        scratch_shapes=[pltpu.VMEM((keys, HD), BF16), pltpu.VMEM((keys, 2 * HD), BF16)],
        compiler_params=params(20),
        cost_estimate=cost(pairs * HD * 4, 4 * queries.size + 8 * kv[0].size, pairs),
        name="attend",
    )(plan, queries, *kv)


def merge(members):
    top = members[0][1]
    for _, lse in members[1:]:
        top = jnp.maximum(top, lse)
    total = 0.0
    out = 0.0
    for part, lse in members:
        w = jnp.exp(lse - top)
        total = total + w
        out = out + part * w
    return out * (1.0 / total), top + jnp.log(total)


def fold_kernel(r_ref, own_ref, lse_ref, far_ref):
    units = own_ref.shape[0]
    rows = 2 * ROWS
    width = lax.axis_size("x")
    lane = lax.broadcasted_iota(jnp.int32, (rows, HD), 1)
    for u in range(units):
        near = jnp.zeros((rows, HD), F32)
        sent = jnp.zeros((rows, HD), F32)
        for g in range(KVH):
            places = [p for p in range(r_ref.shape[0]) if head_of(p // width, p % width) == g]
            tails = []
            for place in places:
                tail = r_ref[place, :, units * GW:].astype(F32)
                first, second, third = (
                    tail[:, (3 * u + i) * GRP:(3 * u + i + 1) * GRP] for i in range(3)
                )
                tails.append(first + second + third)
            for j in range(GRP):
                h = g * GRP + j
                cols = slice(u * GW + j * HD, u * GW + (j + 1) * HD)
                out, lse = merge([
                    (r_ref[place, :, cols].astype(F32), tail[:, j:j + 1])
                    for place, tail in zip(places, tails)
                ])
                own_ref[u, :, h * HD:(h + 1) * HD] = out[:ROWS]
                far_ref[u, :, h * HD:(h + 1) * HD] = out[ROWS:].astype(BF16)
                near = jnp.where(lane == h, lse, near)
                for i, piece in enumerate(split_three(lse)):
                    sent = jnp.where(lane == i * QH + h, piece, sent)
        lse_ref[u] = near[:ROWS]
        far_ref[u, :, QH * HD:] = sent[ROWS:].astype(BF16)


def fold(received, units):
    return pl.pallas_call(
        fold_kernel,
        out_shape=(
            shape((units, ROWS, QH * HD), F32),
            shape((units, ROWS, HD), F32),
            shape((units, ROWS, QH * HD + HD)),
        ),
        compiler_params=params(6),
        cost_estimate=cost(0, 4 * received.size),
        name="fold_plane",
    )(received)


def finish_kernel(own_ref, lse_ref, far_ref, sent_ref, *kept):
    half = QH // 2
    units = own_ref.shape[0]
    for u in reversed(range(units)):
        tail = far_ref[u, :, QH * HD:].astype(F32)
        far_lse = tail[:, :QH] + tail[:, QH:2 * QH] + tail[:, 2 * QH:3 * QH]
        for h in range(QH):
            cols = slice(h * HD, (h + 1) * HD)
            out, _ = merge([
                (own_ref[u, :, cols], lse_ref[u, :, h:h + 1]),
                (far_ref[u, :, cols].astype(F32), far_lse[:, h:h + 1]),
            ])
            out = out.astype(BF16)
            if u < units - 1:
                kept[0][u, :, cols] = out
            else:
                n = h % half
                for chip in range(sent_ref.shape[0] // 2):
                    sent_ref[2 * chip + h // half, :, n * HD:(n + 1) * HD] = out


def finish(own, lse, far):
    units = own.shape[0]
    outs = [shape((lax.axis_size("zl") * lax.axis_size("co"), ROWS, QH * HD // 2))]
    if units > 1:
        outs.append(shape((units - 1,) + own.shape[1:]))
    return pl.pallas_call(
        finish_kernel,
        out_shape=outs,
        compiler_params=params(4),
        cost_estimate=cost(0, 8 * own.size),
        name="finish",
    )(own, lse, far)


def swap(value, axis):
    return lax.ppermute(value, axis, [(0, 1), (1, 0)])


def exchange(value, axes):
    return lax.all_to_all(value, axes, split_axis=0, concat_axis=0, tiled=True)


def across(value, d):
    width = lax.axis_size("x")
    steps = (d & 1) + width * (d >> 1)
    return lax.ppermute(value, PLANE, [(i, i ^ steps) for i in range(width * lax.axis_size("y"))])


def after(value, *earlier):
    return lax.optimization_barrier((value,) + earlier)[0]


def masked_rows(values, masked, filler):
    return jnp.where(masked[..., None] == 1, filler, values)


def body(
    stored_memory,
    opening_probe_vectors,
    opening_memory_pairs,
    opening_hidden_marks,
    second_probe_vectors,
    second_memory_pairs,
    second_hidden_marks,
    continuing_sequence_ids,
    blank_symbol_probe,
    blank_symbol_pairs,
):
    seqs = stored_memory.shape[0]
    wide, pair = QH * HD, 2 * KVH * HD
    plan = make_plan(continuing_sequence_ids, seqs)
    slot_halves = exchange(
        send_slots(
            second_probe_vectors,
            second_memory_pairs,
            second_hidden_marks,
            blank_symbol_probe,
            blank_symbol_pairs,
        ),
        DP,
    )
    query_first = masked_rows(opening_probe_vectors, opening_hidden_marks, blank_symbol_probe)
    block_first = masked_rows(opening_memory_pairs, opening_hidden_marks, blank_symbol_pairs)
    pieces = cut_by_head(stored_memory, block_first)
    kv = [pieces[0]] + [across(piece, d) for d, piece in enumerate(pieces) if d]

    def second_queries(turn, *ahead):
        kept, lent = pick(plan, slot_halves, (SLOT + turn, OTHER + turn))
        return join(kept, swap(lent, "co"), (wide, pair), *ahead)

    def second_member(turn):
        return lambda plan_ref: plan_ref[MEMBER + turn]

    def hand_back(home_halves, *earlier):
        back = after(exchange(home_halves, DP), *earlier)
        kept, lent = pick(plan, back, (HOME, HOME_OTHER))
        return kept, swap(lent, "co")

    def last_pass(early):
        queries, pairs = second_queries(1)
        second_in = exchange(pack(queries, swap(queries, "zh"), pairs), PLANE)
        second_part = attend(plan, second_in, kv, [second_member(1)], seqs)
        own, lse, far = fold(exchange(second_part, PLANE), 1)
        late = hand_back(finish(own, lse, swap(far, "zh"))[0])
        return tuple(jnp.where(plan[WAITS] > 0, new, old) for new, old in zip(late, early))

    queries, pairs = second_queries(0, query_first)
    far = swap(queries, "zh")
    everything = exchange(pack(queries, after(far, *kv[1:]), pairs), PLANE)

    members = list(range(seqs)) + [second_member(0)]
    partial = attend(plan, everything, kv, members, seqs)
    own, lse, far = fold(exchange(partial, PLANE), len(members))
    home_halves, first_out = finish(own, lse, swap(far, "zh"))
    shared = plan[SHARED] > 0
    halves = hand_back(home_halves, shared)
    halves = lax.cond(shared, last_pass, lambda early: early, halves)
    return first_out, join(*halves, (wide,))[0]


def solution(mesh):
    fine = Mesh(mesh.devices.reshape(8, 2, 2, 4, 4), ("zl", "co", "zh", "y", "x"))
    rows = P(DP, CTX, None)
    marks = P(DP, CTX)
    return jax.shard_map(
        body,
        mesh=fine,
        in_specs=(rows, rows, rows, marks, rows, rows, marks, P(), P(), P()),
        out_specs=(rows, rows),
        check_vma=False,
    )
```

```python
import functools

import jax
import jax.numpy as jnp
from jax import lax
from jax.experimental import pallas as pl
from jax.experimental.pallas import tpu as pltpu
from jax.sharding import Mesh, PartitionSpec as P

QH = 16
KVH = 4
HD = 128
GRP = QH // KVH
GW = GRP * HD
ROWS = 8
DP = ("zl", "co")
PLANE = ("y", "x")
CTX = ("zh", "y", "x")
SCALE = HD ** -0.5
LOG2E = 1.4426950408889634
F32 = jnp.float32
BF16 = jnp.bfloat16


def cost(flops, nbytes, trans=0):
    return pl.CostEstimate(flops=flops, bytes_accessed=nbytes, transcendentals=trans)


def params(mib):
    return pltpu.CompilerParams(vmem_limit_bytes=mib * 2 ** 20)


def shape(dims, dtype=BF16):
    return jax.ShapeDtypeStruct(dims, dtype)


def in_smem():
    return pl.BlockSpec(memory_space=pltpu.SMEM)


def in_vmem():
    return pl.BlockSpec(memory_space=pltpu.VMEM)


def split_three(v):
    hi = v.astype(BF16)
    rest = v - hi.astype(F32)
    mid = rest.astype(BF16)
    low = (rest - mid.astype(F32)).astype(BF16)
    return hi.astype(F32), mid.astype(F32), low.astype(F32)


SLOT, OTHER, MEMBER, HOME, HOME_OTHER, SHARED, WAITS = 0, 2, 4, 6, 7, 8, 9


def plan_kernel(seqs, ids_ref, o_ref):
    count = ids_ref.shape[0]
    core = lax.axis_index("co")
    group = lax.axis_index("zl") * lax.axis_size("co") + core
    other = group + 1 - 2 * core
    for where, place in ((group, SLOT), (other, OTHER)):
        seen = jnp.int32(0)
        slot = [jnp.int32(0), jnp.int32(0)]
        member = [jnp.int32(0), jnp.int32(0)]
        for j in range(count):
            one = ids_ref[j]
            home = lax.div(one, jnp.int32(seqs))
            hit = home == where
            for turn in range(2):
                now = hit & (seen == turn)
                slot[turn] = jnp.where(now, j, slot[turn])
                member[turn] = jnp.where(now, one - home * seqs, member[turn])
            seen = seen + hit.astype(jnp.int32)
        for turn in range(2):
            o_ref[place + turn] = slot[turn]
            if place == SLOT:
                o_ref[MEMBER + turn] = member[turn]
    taken, shared, waits = jnp.int32(0), jnp.int32(0), jnp.int32(0)
    for j in range(count):
        bit = lax.shift_left(jnp.int32(1), lax.div(ids_ref[j], jnp.int32(seqs)))
        second = ((taken & bit) != 0).astype(jnp.int32)
        shared = shared | second
        waits = jnp.where(group == j, second, waits)
        taken = taken | bit
    o_ref[SHARED] = shared
    o_ref[WAITS] = waits
    o_ref[HOME] = lax.div(ids_ref[group], jnp.int32(seqs))
    o_ref[HOME_OTHER] = lax.div(ids_ref[other], jnp.int32(seqs))


def make_plan(ids, seqs):
    return pl.pallas_call(
        functools.partial(plan_kernel, seqs),
        in_specs=[in_smem()],
        out_specs=in_smem(),
        out_shape=shape((10,), jnp.int32),
        compiler_params=params(1),
        cost_estimate=cost(0, 128),
        name="plan",
    )(ids)


def head_of(y, x):
    return 2 * (y & 1) + (x & 1)


def own_head():
    return head_of(lax.axis_index("y"), lax.axis_index("x"))


def cut_kernel(s_ref, b_ref, *outs):
    here = own_head()
    seqs, rows, _ = s_ref.shape
    for d, out in enumerate(outs):
        head = jnp.bitwise_xor(here, d)
        for part in range(2):
            columns = pl.ds(pl.multiple_of((part * KVH + head) * HD, HD), HD)
            cols = slice(part * HD, (part + 1) * HD)
            for n in range(seqs):
                out[n * rows:(n + 1) * rows, cols] = s_ref[n, :, columns]
            blocks = [b_ref[n, :, columns].astype(F32) for n in range(seqs)]
            out[seqs * rows:, cols] = jnp.concatenate(blocks, axis=0).astype(BF16)


def cut_by_head(stored, blocks):
    seqs, rows, _ = stored.shape
    return pl.pallas_call(
        cut_kernel,
        out_shape=[shape((seqs * (rows + ROWS), 2 * HD))] * KVH,
        compiler_params=params(12),
        cost_estimate=cost(0, 4 * stored.size),
        name="cut_by_head",
    )(stored, blocks)


def send_kernel(*refs):
    given, o_ref, held, sem = refs[:5], refs[5], refs[6:11], refs[11]
    copies = [pltpu.make_async_copy(a, b, sem.at[n]) for n, (a, b) in enumerate(zip(given, held))]
    for copy in copies:
        copy.start()
    for copy in copies:
        copy.wait()
    q_ref, kv_ref, mark_ref, bq_ref, bkv_ref = held
    square = (ROWS, ROWS)
    eye = lax.broadcasted_iota(jnp.int32, square, 0) == lax.broadcasted_iota(jnp.int32, square, 1)
    marks = jnp.broadcast_to(mark_ref[...], square)
    column = jnp.sum(jnp.where(eye, marks, 0).astype(F32), axis=1, keepdims=True)
    hidden = jnp.broadcast_to(column == 1.0, (ROWS, HD))
    for blank, values, first in ((bq_ref, q_ref, 0), (bkv_ref, kv_ref, q_ref.shape[2] // 2)):
        half = values.shape[2] // 2
        for c in range(2):
            value = jnp.concatenate(
                [
                    jnp.where(
                        hidden,
                        jnp.broadcast_to(blank[i:i + 1].astype(F32), (ROWS, HD)),
                        values[0, :, i * HD:(i + 1) * HD].astype(F32),
                    )
                    for i in range(c * half // HD, (c + 1) * half // HD)
                ],
                axis=1,
            ).astype(BF16)
            for chip in range(o_ref.shape[0] // 2):
                o_ref[2 * chip + c, :, first:first + half] = value


def send_slots(q, kv, marks, blank_q, blank_kv):
    groups = lax.axis_size("zl") * lax.axis_size("co")
    out = shape((groups, ROWS, (q.shape[2] + kv.shape[2]) // 2))
    given = (q, kv, marks, blank_q.reshape(-1, HD), blank_kv.reshape(-1, HD))
    return pl.pallas_call(
        send_kernel,
        in_specs=[pl.BlockSpec(memory_space=pltpu.HBM)] * len(given),
        out_specs=in_vmem(),
        out_shape=out,
        scratch_shapes=[pltpu.VMEM(value.shape, value.dtype) for value in given]
        + [pltpu.SemaphoreType.DMA((len(given),))],
        cost_estimate=cost(0, 2 * out.size),
        name="send_slots",
    )(*given)


def pick_kernel(entries, plan_ref, halves_ref, *outs):
    for entry, out in zip(entries, outs):
        out[0] = halves_ref[plan_ref[entry]]


def pick(plan, halves, entries):
    return pl.pallas_call(
        functools.partial(pick_kernel, entries),
        in_specs=[in_smem(), in_vmem()],
        out_specs=[in_vmem()] * len(entries),
        out_shape=[shape((1,) + halves.shape[1:])] * len(entries),
        compiler_params=params(2),
        cost_estimate=cost(0, 4 * halves.size),
        name="pick",
    )(plan, halves)


def join_kernel(given, kept_ref, got_ref, *refs):
    aheads, outs = refs[:given], refs[given:]
    low = lax.axis_index("co") == 0
    first = 0
    for n, out in enumerate(outs):
        last = out.shape[0] - 1
        if n < given:
            out[:last] = aheads[n][...]
        half = out.shape[2] // 2
        cols = slice(first, first + half)

        @pl.when(low)
        def _(out=out, last=last, half=half, cols=cols):
            out[last, :, :half] = kept_ref[0, :, cols]
            out[last, :, half:] = got_ref[0, :, cols]

        @pl.when(jnp.logical_not(low))
        def _(out=out, last=last, half=half, cols=cols):
            out[last, :, :half] = got_ref[0, :, cols]
            out[last, :, half:] = kept_ref[0, :, cols]

        first += half


def join(kept, got, widths, *aheads):
    ahead = [value.shape[0] for value in aheads] + [0] * (len(widths) - len(aheads))
    return pl.pallas_call(
        functools.partial(join_kernel, len(aheads)),
        out_shape=[shape((units + 1, ROWS, width)) for units, width in zip(ahead, widths)],
        compiler_params=params(2),
        cost_estimate=cost(0, 8 * kept.size),
        name="join",
    )(kept, got, *aheads)


def pack_kernel(own_ref, both_ref, kv_ref, o_ref):
    far_ref = both_ref.at[1 - lax.axis_index("zh")]
    width = lax.axis_size("x")
    units = own_ref.shape[0]
    for h in range(KVH):
        cols = slice(h * GW, (h + 1) * GW)
        values = [
            jnp.concatenate(
                [own_ref[u, :, cols].astype(F32), far_ref[u, :, cols].astype(F32)], axis=0
            ).astype(BF16)
            for u in range(units)
        ]
        k = kv_ref[0, :, h * HD:(h + 1) * HD].astype(F32)
        v = kv_ref[0, :, (KVH + h) * HD:(KVH + h + 1) * HD].astype(F32)
        kv = jnp.concatenate([k, v], axis=0).astype(BF16)
        for place in range(o_ref.shape[0]):
            if head_of(place // width, place % width) == h:
                for u, value in enumerate(values):
                    o_ref[place, :, u * GW:(u + 1) * GW] = value
                o_ref[place, :, units * GW:] = kv


def pack(own, far, kv):
    places = lax.axis_size("y") * lax.axis_size("x")
    out = shape((places, 2 * ROWS, own.shape[0] * GW + HD))
    return pl.pallas_call(
        pack_kernel,
        out_shape=out,
        compiler_params=params(6),
        cost_estimate=cost(0, 2 * out.size),
        name="pack_queries",
    )(own, far, kv)


def attend_kernel(members, seqs, plan_ref, q_ref, *refs):
    kv_refs, o_ref, k_all, v_all = refs[:KVH], refs[KVH], refs[KVH + 1], refs[KVH + 2]
    places, units = o_ref.shape[0], len(members)
    rows = places * 2 * ROWS
    span = kv_refs[0].shape[0] // seqs - ROWS
    cached = KVH * span
    y, x = lax.axis_index("y"), lax.axis_index("x")
    width = lax.axis_size("x")
    corner = (y - (y & 1)) * width + x - (x & 1)
    lane = lax.broadcasted_iota(jnp.int32, (rows, HD), 1)
    stats = jnp.zeros((rows, HD), F32)
    v_all[:, HD:] = jnp.ones((cached + KVH * ROWS, HD), BF16)
    for u, member in enumerate(members):
        if isinstance(member, int):
            blocks = [kv_ref[seqs * span:].astype(F32) for kv_ref in kv_refs]
            own = slice(member * ROWS, (member + 1) * ROWS)
            near = [(block[own, :HD], block[own, HD:]) for block in blocks]
            start = member * span
        else:
            blocks = [
                q_ref[corner + dy * width + dx, :, units * GW:].astype(F32)
                for dy in range(2)
                for dx in range(2)
            ]
            near = [(block[:ROWS], block[ROWS:]) for block in blocks]
            start = pl.multiple_of(member(plan_ref) * span, span)
        for n, kv_ref in enumerate(kv_refs):
            k_all[n * span:(n + 1) * span] = kv_ref[pl.ds(start, span), :HD]
            v_all[n * span:(n + 1) * span, :HD] = kv_ref[pl.ds(start, span), HD:]
        k_all[cached:] = jnp.concatenate([k for k, _ in near], axis=0).astype(BF16)
        v_all[cached:, :HD] = jnp.concatenate([v for _, v in near], axis=0).astype(BF16)
        for j in range(GRP):
            cols = slice(u * GW + j * HD, u * GW + (j + 1) * HD)
            q = q_ref[:, :, cols].reshape(rows, HD)
            scores = lax.dot_general(
                q, k_all[...], (((1,), (1,)), ((), ())), preferred_element_type=F32
            )
            top = jnp.max(scores, axis=1, keepdims=True)
            w = jnp.exp2((scores - top) * (SCALE * LOG2E))
            both = jnp.dot(w.astype(BF16), v_all[...], preferred_element_type=F32)
            total = both[:, HD:]
            out = both[:, :HD] * (1.0 / total)
            o_ref[:, :, cols] = out.astype(BF16).reshape(places, 2 * ROWS, HD)
            for i, piece in enumerate(split_three(top * SCALE + jnp.log(total))):
                stats = jnp.where(lane == (3 * u + i) * GRP + j, piece, stats)
    o_ref[:, :, units * GW:] = stats.astype(BF16).reshape(places, 2 * ROWS, HD)


def attend(plan, queries, kv, members, seqs):
    places, units = queries.shape[0], len(members)
    keys = KVH * (kv[0].shape[0] // seqs)
    pairs = units * places * 2 * ROWS * GRP * keys
    return pl.pallas_call(
        functools.partial(attend_kernel, members, seqs),
        in_specs=[in_smem()] + [in_vmem()] * (1 + KVH),
        out_specs=in_vmem(),
        out_shape=shape(queries.shape),
        scratch_shapes=[pltpu.VMEM((keys, HD), BF16), pltpu.VMEM((keys, 2 * HD), BF16)],
        compiler_params=params(20),
        cost_estimate=cost(pairs * HD * 4, 4 * queries.size + 8 * kv[0].size, pairs),
        name="attend",
    )(plan, queries, *kv)


def merge(members):
    top = members[0][1]
    for _, lse in members[1:]:
        top = jnp.maximum(top, lse)
    total = 0.0
    out = 0.0
    for part, lse in members:
        w = jnp.exp(lse - top)
        total = total + w
        out = out + part * w
    return out * (1.0 / total), top + jnp.log(total)


def fold_kernel(r_ref, own_ref, lse_ref, far_ref):
    units = own_ref.shape[0]
    rows = 2 * ROWS
    width = lax.axis_size("x")
    lane = lax.broadcasted_iota(jnp.int32, (rows, HD), 1)
    for u in range(units):
        near = jnp.zeros((rows, HD), F32)
        sent = jnp.zeros((rows, HD), F32)
        for g in range(KVH):
            places = [p for p in range(r_ref.shape[0]) if head_of(p // width, p % width) == g]
            tails = []
            for place in places:
                tail = r_ref[place, :, units * GW:].astype(F32)
                first, second, third = (
                    tail[:, (3 * u + i) * GRP:(3 * u + i + 1) * GRP] for i in range(3)
                )
                tails.append(first + second + third)
            for j in range(GRP):
                h = g * GRP + j
                cols = slice(u * GW + j * HD, u * GW + (j + 1) * HD)
                out, lse = merge([
                    (r_ref[place, :, cols].astype(F32), tail[:, j:j + 1])
                    for place, tail in zip(places, tails)
                ])
                own_ref[u, :, h * HD:(h + 1) * HD] = out[:ROWS]
                far_ref[u, :, h * HD:(h + 1) * HD] = out[ROWS:].astype(BF16)
                near = jnp.where(lane == h, lse, near)
                for i, piece in enumerate(split_three(lse)):
                    sent = jnp.where(lane == i * QH + h, piece, sent)
        lse_ref[u] = near[:ROWS]
        far_ref[u, :, QH * HD:] = sent[ROWS:].astype(BF16)


def fold(received, units):
    return pl.pallas_call(
        fold_kernel,
        out_shape=(
            shape((units, ROWS, QH * HD), F32),
            shape((units, ROWS, HD), F32),
            shape((units, ROWS, QH * HD + HD)),
        ),
        compiler_params=params(6),
        cost_estimate=cost(0, 4 * received.size),
        name="fold_plane",
    )(received)


def finish_kernel(own_ref, lse_ref, both_ref, sent_ref, *kept):
    far_ref = both_ref.at[1 - lax.axis_index("zh")]
    half = QH // 2
    units = own_ref.shape[0]
    for u in reversed(range(units)):
        tail = far_ref[u, :, QH * HD:].astype(F32)
        far_lse = tail[:, :QH] + tail[:, QH:2 * QH] + tail[:, 2 * QH:3 * QH]
        for h in range(QH):
            cols = slice(h * HD, (h + 1) * HD)
            out, _ = merge([
                (own_ref[u, :, cols], lse_ref[u, :, h:h + 1]),
                (far_ref[u, :, cols].astype(F32), far_lse[:, h:h + 1]),
            ])
            out = out.astype(BF16)
            if u < units - 1:
                kept[0][u, :, cols] = out
            else:
                n = h % half
                for chip in range(sent_ref.shape[0] // 2):
                    sent_ref[2 * chip + h // half, :, n * HD:(n + 1) * HD] = out


def finish(own, lse, far):
    units = own.shape[0]
    outs = [shape((lax.axis_size("zl") * lax.axis_size("co"), ROWS, QH * HD // 2))]
    if units > 1:
        outs.append(shape((units - 1,) + own.shape[1:]))
    return pl.pallas_call(
        finish_kernel,
        out_shape=outs,
        compiler_params=params(4),
        cost_estimate=cost(0, 8 * own.size),
        name="finish",
    )(own, lse, far)


def swap(value, axis):
    return lax.ppermute(value, axis, [(0, 1), (1, 0)])


def exchange(value, axes):
    return lax.all_to_all(value, axes, split_axis=0, concat_axis=0, tiled=True)


def across(value, d):
    width = lax.axis_size("x")
    steps = (d & 1) + width * (d >> 1)
    return lax.ppermute(value, PLANE, [(i, i ^ steps) for i in range(width * lax.axis_size("y"))])


def both_z(value):
    return lax.all_gather(value, "zh", axis=0)


def after(value, *earlier):
    return lax.optimization_barrier((value,) + earlier)[0]


def masked_rows(values, masked, filler):
    return jnp.where(masked[..., None] == 1, filler, values)


def body(
    stored_memory,
    opening_probe_vectors,
    opening_memory_pairs,
    opening_hidden_marks,
    second_probe_vectors,
    second_memory_pairs,
    second_hidden_marks,
    continuing_sequence_ids,
    blank_symbol_probe,
    blank_symbol_pairs,
):
    seqs = stored_memory.shape[0]
    wide, pair = QH * HD, 2 * KVH * HD
    plan = make_plan(continuing_sequence_ids, seqs)
    slot_halves = exchange(
        send_slots(
            second_probe_vectors,
            second_memory_pairs,
            second_hidden_marks,
            blank_symbol_probe,
            blank_symbol_pairs,
        ),
        DP,
    )
    query_first = masked_rows(opening_probe_vectors, opening_hidden_marks, blank_symbol_probe)
    block_first = masked_rows(opening_memory_pairs, opening_hidden_marks, blank_symbol_pairs)
    pieces = cut_by_head(stored_memory, block_first)
    kv = [pieces[0]] + [across(piece, d) for d, piece in enumerate(pieces) if d]

    def second_queries(turn, *ahead):
        kept, lent = pick(plan, slot_halves, (SLOT + turn, OTHER + turn))
        return join(kept, swap(lent, "co"), (wide, pair), *ahead)

    def second_member(turn):
        return lambda plan_ref: plan_ref[MEMBER + turn]

    def hand_back(home_halves, *earlier):
        back = after(exchange(home_halves, DP), *earlier)
        kept, lent = pick(plan, back, (HOME, HOME_OTHER))
        return kept, swap(lent, "co")

    def last_pass(early):
        queries, pairs = second_queries(1)
        second_in = exchange(pack(queries, both_z(queries), pairs), PLANE)
        second_part = attend(plan, second_in, kv, [second_member(1)], seqs)
        own, lse, far = fold(exchange(second_part, PLANE), 1)
        late = hand_back(finish(own, lse, both_z(far))[0])
        return tuple(jnp.where(plan[WAITS] > 0, new, old) for new, old in zip(late, early))

    queries, pairs = second_queries(0, query_first)
    far = both_z(queries)
    everything = exchange(pack(queries, after(far, *kv[1:]), pairs), PLANE)

    members = list(range(seqs)) + [second_member(0)]
    partial = attend(plan, everything, kv, members, seqs)
    own, lse, far = fold(exchange(partial, PLANE), len(members))
    home_halves, first_out = finish(own, lse, both_z(far))
    shared = plan[SHARED] > 0
    halves = hand_back(home_halves, shared)
    halves = lax.cond(shared, last_pass, lambda early: early, halves)
    return first_out, join(*halves, (wide,))[0]


def solution(mesh):
    fine = Mesh(mesh.devices.reshape(8, 2, 2, 4, 4), ("zl", "co", "zh", "y", "x"))
    rows = P(DP, CTX, None)
    marks = P(DP, CTX)
    return jax.shard_map(
        body,
        mesh=fine,
        in_specs=(rows, rows, rows, marks, rows, rows, marks, P(), P(), P()),
        out_specs=(rows, rows),
        check_vma=False,
    )
```
